512 devices in a mesh: dp: 32 (over x, z), group: 2 (over core), mp: 8 (over y).
Axes of the slice: x: 4, y: 8, z: 8, core: 2. Of those that a mesh axis runs over, the one named last changes fastest.
Arguments:
- teacher_rows: bfloat16 [20480, 5120], P('dp', ('group', 'mp')), may hold values from -500 to 500
- teacher_gain: bfloat16 [5120], P(('group', 'mp')), may hold values from 0.099609375 to 1.8984375
- teacher_head: bfloat16 [6144, 5120], P(('group', 'mp'), 'dp'), may hold values from -3 to 3
- student_rows: bfloat16 [20480, 2048], P('dp'), may hold values from -500 to 500
- student_gain: bfloat16 [2048], replicated, may hold values from 0.099609375 to 1.8984375
- student_head: bfloat16 [6144, 2048], P(('group', 'mp'), 'dp'), may hold values from -3 to 3
- lengths: int32 [32], P('dp'), may hold values from 384 to 640, as said below
Outputs:
- head_update: bfloat16 [6144, 2048], P(('group', 'mp'), 'dp')
- row_update: bfloat16 [20480, 2048], P(('dp', 'group', 'mp'))
The draws below stay inside these ranges and needn't reach their ends.
Inputs may be any that keep to these rules, and one draw needn't show every extreme that they name: `lengths`: the first sequence has exactly 384 tokens and the last exactly 640.
All inputs are finite; a program needn't handle non-finite values.
Results may differ from the reference program's by a relative error of at most 0.023.
Values may be sent and summed in bfloat16 or wider, within the bound.
No kernel may reach another device: no remote copies, remote signals or barrier semaphores. Data moves between devices by JAX's collectives and lax.ppermute only.
A program may use at most 64 MiB of HBM per device.

```python
import math
import jax
import jax.numpy as jnp
from jax import lax

DT = 5120
DS = 2048
VOC_DEV = 384
LMAX = 640
SEQ_DEV = 1
TOK_DEV = 640
SEQUENCES = 32
TOKENS = 20480
VOCAB = 6144
N_DP = 32
N_GROUP = 2
N_MP = 8


def spread_scales(key, rows, cols):
    key_row, key_col = jax.random.split(key)
    row_scale = jnp.exp(jax.random.uniform(key_row, (rows, 1), minval=0.0, maxval=math.log(10.0)))
    col_scale = jnp.exp(jax.random.uniform(key_col, (1, cols), minval=0.0, maxval=math.log(10.0)))
    return row_scale * col_scale


def drawn_rows(key, width):
    key_value, key_scale = jax.random.split(key)
    values = jax.random.truncated_normal(key_value, -4.0, 4.0, (TOKENS, width))
    return values * spread_scales(key_scale, TOKENS, width)


def head_values(key, width):
    return jax.random.truncated_normal(key, -4.0, 4.0, (VOCAB, width)) * (3.0 / math.sqrt(width))


def draw_teacher_rows(key, part):
    key = jax.random.fold_in(key, 11)
    values = drawn_rows(key, DT)
    return values.astype(jnp.bfloat16)


def draw_teacher_head(key, part):
    key = jax.random.fold_in(key, 12)
    values = head_values(key, DT)
    return values.astype(jnp.bfloat16)


def draw_student_rows(key, part):
    key = jax.random.fold_in(key, 14)
    values = drawn_rows(key, DS)
    return values.astype(jnp.bfloat16)


def draw_student_head(key, part):
    key = jax.random.fold_in(key, 15)
    values = head_values(key, DS)
    return values.astype(jnp.bfloat16)


def draw_lengths(key, part):
    key = jax.random.fold_in(key, 13)
    shortest = 3 * LMAX // 5
    reach = LMAX // 8
    climb = 2 * LMAX // 5 - reach
    index = jnp.arange(SEQUENCES, dtype=jnp.int32)
    base = shortest + climb * index // SEQUENCES
    values = base + jax.random.randint(key, (SEQUENCES,), 0, reach + 1, dtype=jnp.int32)
    values = jnp.minimum(values, LMAX)
    values = values.at[0].set(shortest)
    return values.at[SEQUENCES - 1].set(LMAX)


def setup_inputs(seed: int = 0) -> dict:
    streams_of = jax.random.split(jax.random.key(seed), 8)
    return {
        "teacher_rows": draw_teacher_rows(jax.random.fold_in(streams_of[7], 71), 0),
        "teacher_gain": jnp.clip(1.0 + 0.18 * jax.random.normal(streams_of[1], (DT,), jnp.float32), 0.099609375, 1.8984375).astype(jnp.bfloat16),
        "teacher_head": draw_teacher_head(jax.random.fold_in(streams_of[7], 71), 0),
        "student_rows": draw_student_rows(jax.random.fold_in(streams_of[7], 71), 0),
        "student_gain": jnp.clip(1.0 + 0.18 * jax.random.normal(streams_of[4], (DS,), jnp.float32), 0.099609375, 1.8984375).astype(jnp.bfloat16),
        "student_head": draw_student_head(jax.random.fold_in(streams_of[7], 71), 0),
        "lengths": draw_lengths(jax.random.fold_in(streams_of[7], 71), 0),
    }


epsilon = 1e-06

def rms_rows(rows, gain):
    values = rows.astype(jnp.float32)
    mean_square = lax.optimization_barrier(jnp.mean(values * values, axis=-1, keepdims=True))
    return (values * lax.rsqrt(mean_square + epsilon) * gain.astype(jnp.float32)).astype(jnp.bfloat16)

def log_total(logits):
    highest = lax.optimization_barrier(jnp.max(logits, axis=1))
    return highest + jnp.log(lax.optimization_barrier(jnp.sum(jnp.exp(logits - highest[:, None]), axis=1)))

def to_bfloat(values):
    rounded = values.astype(jnp.bfloat16)
    rounded = lax.optimization_barrier(rounded)
    return rounded.astype(jnp.float32)

def reference(teacher_rows, teacher_gain, teacher_head, student_rows, student_gain, student_head, lengths):
    shards = N_GROUP * N_MP
    teacher_normed = rms_rows(teacher_rows, teacher_gain).reshape(N_DP, TOK_DEV, DT)
    student_normed = rms_rows(student_rows, student_gain).reshape(N_DP, TOK_DEV, DS)
    position = jnp.arange(TOK_DEV, dtype=jnp.int32) % LMAX
    owner_lengths = lengths.reshape(N_DP, SEQ_DEV)
    head_blocks = student_head.reshape(shards, VOC_DEV, DS).astype(jnp.float32)

    def group_step(head_total, inputs):
        teacher_block, student_block, seq_lengths = inputs
        live = (position < jnp.repeat(seq_lengths, LMAX, total_repeat_length=TOK_DEV)).astype(jnp.float32)
        teacher_logits = jnp.dot(teacher_block, teacher_head.T, preferred_element_type=jnp.float32)
        student_logits = jnp.dot(student_block, student_head.T, preferred_element_type=jnp.float32)
        teacher_lse = log_total(teacher_logits)
        student_lse = log_total(student_logits)
        teacher_prob = jnp.exp(teacher_logits - teacher_lse[:, None])
        student_prob = jnp.exp(student_logits - student_lse[:, None])
        logit_grad = (live[:, None] * (student_prob - teacher_prob)).astype(jnp.bfloat16)
        head_part = to_bfloat(jnp.dot(logit_grad.T, student_block, preferred_element_type=jnp.float32))
        grad_blocks = logit_grad.astype(jnp.float32).reshape(TOK_DEV, shards, VOC_DEV)
        row_parts = jnp.einsum('tnv,nvd->ntd', grad_blocks, head_blocks, precision=lax.Precision.HIGHEST)
        row_grad = lax.optimization_barrier(jnp.sum(to_bfloat(row_parts), axis=0))
        return (head_total + head_part, row_grad)
    head_grad, row_grad = lax.scan(group_step, jnp.zeros((VOCAB, DS), jnp.float32), (teacher_normed, student_normed, owner_lengths))
    row_grad = row_grad.reshape(TOKENS, DS)
    head_update = (head_grad * lax.rsqrt(jnp.mean(head_grad * head_grad) + epsilon)).astype(jnp.bfloat16)
    row_update = (row_grad * lax.rsqrt(jnp.mean(row_grad * row_grad) + epsilon)).astype(jnp.bfloat16)
    return (head_update, row_update)
```

```python
import jax
import jax.numpy as jnp
from jax import lax
from jax.sharding import Mesh, PartitionSpec as P

F32 = jnp.float32
BF16 = jnp.bfloat16
DT = 5120
NX, NZ, NC, NY = 4, 8, 2, 8
epsilon = 1e-06


def split3(values):
    high = values.astype(BF16)
    rest = values - high.astype(F32)
    middle = rest.astype(BF16)
    low = (rest - middle.astype(F32)).astype(BF16)
    return high, middle, low


def normalize(rows, gain):
    values = rows.astype(F32)
    mean_square = jnp.mean(values * values, axis=-1, keepdims=True)
    return (values * lax.rsqrt(mean_square + epsilon) * gain.astype(F32)).astype(BF16)


def shifted(values, axis, size, by):
    return lax.ppermute(values, axis, [(i, (i + by) % size) for i in range(size)])


def body(
    teacher_rows, teacher_gain, teacher_head, student_rows, student_gain, student_head, lengths
):
    tokens = student_rows.shape[0]
    ft, fs = teacher_head.shape[1], student_head.shape[1]
    vocab = teacher_head.shape[0]
    z = lax.axis_index("z")
    c = lax.axis_index("core")

    block = teacher_rows.T
    wide = block.shape[0]
    values = block.astype(F32)
    scaled = (values * teacher_gain.astype(F32)[:, None]).astype(BF16)
    squares = jnp.stack(split3(jnp.sum(values * values, axis=0)), axis=0)
    sent = jnp.concatenate([scaled, jnp.pad(squares, ((0, 13), (0, 0)))], axis=0)
    rows = lax.all_gather(sent, ("core", "y"), axis=0, tiled=False)

    heads = jnp.concatenate([student_head.T, teacher_head.T], axis=0)
    own = lax.all_gather(heads, "x", axis=0, tiled=False)
    student_w = jnp.zeros((NX, NZ, fs, vocab), BF16)
    teacher_w = jnp.zeros((NX, NZ, ft, vocab), BF16)

    def place(ws, part, at):
        s, t = ws
        s = lax.dynamic_update_slice(s, part[:, None, :fs], (0, at, 0, 0))
        t = lax.dynamic_update_slice(t, part[:, None, fs:], (0, at, 0, 0))
        return s, t

    ws = place((student_w, teacher_w), own, z)
    right = left = own
    for step in range(1, NZ // 2 + 1):
        right = shifted(right, "z", NZ, 1)
        if step < NZ // 2:
            left = shifted(left, "z", NZ, -1)
        ws = place(ws, right, (z - step) % NZ)
        if step < NZ // 2:
            ws = place(ws, left, (z + step) % NZ)
    student_w = ws[0].reshape(NX * NZ * fs, vocab)
    teacher_w = ws[1].reshape(NC * NY, wide, vocab)

    student_normed = normalize(student_rows, student_gain)
    student_logits = jnp.dot(student_normed, student_w, preferred_element_type=F32)
    total = jnp.sum(rows[:, wide : wide + 3].astype(F32), axis=(0, 1))
    scale = lax.rsqrt(total / DT + epsilon)
    teacher_logits = (
        lax.dot_general(
            rows[:, :wide],
            teacher_w,
            (((0, 1), (0, 1)), ((), ())),
            preferred_element_type=F32,
        )
        * scale[:, None]
    )

    tops = [jnp.max(v, axis=1) for v in (teacher_logits, student_logits)]
    sums = [
        jnp.sum(jnp.exp(v - top[:, None]), axis=1)
        for v, top in zip((teacher_logits, student_logits), tops)
    ]
    stats = jnp.stack(tops + sums, axis=0)
    stats = jnp.broadcast_to(stats[None], (NC * NY,) + stats.shape)
    stats = lax.all_to_all(stats, ("core", "y"), 0, 0, tiled=True)
    top = jnp.max(stats[:, :2], axis=0)
    lse = top + jnp.log(jnp.sum(stats[:, 2:] * jnp.exp(stats[:, :2] - top), axis=0))
    live = (jnp.arange(tokens, dtype=jnp.int32) < lengths[0]).astype(F32)
    logit_grad = (
        live[:, None]
        * (jnp.exp(student_logits - lse[1][:, None]) - jnp.exp(teacher_logits - lse[0][:, None]))
    ).astype(BF16)

    row_part = lax.dot_general(
        logit_grad, student_w, (((1,), (1,)), ((), ())), preferred_element_type=F32
    )
    half = tokens // NC
    mine = lax.dynamic_slice_in_dim(row_part, c * half, half, 0)
    other = lax.dynamic_slice_in_dim(row_part, (1 - c) * half, half, 0).astype(BF16)
    mine = (mine + lax.ppermute(other, "core", [(0, 1), (1, 0)]).astype(F32)).astype(BF16)
    row_grad = lax.psum_scatter(mine, "y", scatter_dimension=0, tiled=True).astype(F32)

    head_part = lax.dot_general(
        student_normed, logit_grad, (((0,), (0,)), ((), ())), preferred_element_type=F32
    ).astype(BF16)
    head_part = lax.all_to_all(head_part.reshape(NX, NZ * fs, vocab), "x", 0, 0, tiled=True)
    head_part = jnp.sum(head_part.astype(F32), axis=0).astype(BF16)
    head_part = lax.all_to_all(head_part.reshape(NZ, fs, vocab), "z", 0, 0, tiled=True)
    head_grad = jnp.sum(head_part.astype(F32), axis=0)

    devices = NX * NZ * NC * NY
    squares = jnp.stack([jnp.sum(head_grad * head_grad), jnp.sum(row_grad * row_grad)])
    squares = jnp.broadcast_to(squares[None, :, None], (devices, 2, 64)).reshape(devices, 128)
    squares = lax.all_to_all(squares, ("x", "z", "core", "y"), 0, 0, tiled=True)
    squares = jnp.sum(squares, axis=0)
    head_update = head_grad * lax.rsqrt(squares[0] / (head_grad.size * devices) + epsilon)
    row_update = row_grad * lax.rsqrt(squares[64] / (row_grad.size * devices) + epsilon)
    return (head_update.astype(BF16).T, row_update.astype(BF16))


def solution(mesh):
    mesh = Mesh(mesh.devices.reshape(NX, NZ, NC, NY), ("x", "z", "core", "y"))
    dp, mp = ("x", "z"), ("core", "y")
    placed = (P(dp, mp), P(mp), P(mp, dp), P(dp, None), P(), P(mp, dp), P(dp))
    return jax.shard_map(
        body,
        mesh=mesh,
        in_specs=placed,
        out_specs=(P(mp, dp), P(dp + mp, None)),
        check_vma=False,
    )
```

```python
import jax
import jax.numpy as jnp
from jax import lax
from jax.sharding import Mesh, PartitionSpec as P

F32 = jnp.float32
BF16 = jnp.bfloat16
DT = 5120
NX, NZ, NC, NY = 4, 8, 2, 8
epsilon = 1e-06


def split3(values):
    high = values.astype(BF16)
    rest = values - high.astype(F32)
    middle = rest.astype(BF16)
    low = (rest - middle.astype(F32)).astype(BF16)
    return high, middle, low


def normalize(rows, gain):
    values = rows.astype(F32)
    mean_square = jnp.mean(values * values, axis=-1, keepdims=True)
    return (values * lax.rsqrt(mean_square + epsilon) * gain.astype(F32)).astype(BF16)


def shifted(values, axis, size, by):
    return lax.ppermute(values, axis, [(i, (i + by) % size) for i in range(size)])


def body(
    teacher_rows, teacher_gain, teacher_head, student_rows, student_gain, student_head, lengths
):
    tokens = student_rows.shape[0]
    ft, fs = teacher_head.shape[1], student_head.shape[1]
    vocab = teacher_head.shape[0]
    x, z = lax.axis_index("x"), lax.axis_index("z")
    c = lax.axis_index("core")

    block = teacher_rows.T
    wide = block.shape[0]
    values = block.astype(F32)
    scaled = (values * teacher_gain.astype(F32)[:, None]).astype(BF16)
    squares = jnp.stack(split3(jnp.sum(values * values, axis=0)), axis=0)
    sent = jnp.concatenate([scaled, jnp.pad(squares, ((0, 13), (0, 0)))], axis=0)
    rows = lax.all_gather(sent, ("core", "y"), axis=0, tiled=False)

    first = ft * 2 // 5
    part_a = jnp.concatenate([student_head.T, teacher_head.T[:first]], axis=0)
    part_b = teacher_head.T[first:]
    own_a = lax.all_gather(part_a, "x", axis=0, tiled=False)
    own_b = lax.all_gather(part_b, "z", axis=0, tiled=False)
    student_w = jnp.zeros((NX, NZ, fs, vocab), BF16)
    teacher_w = jnp.zeros((NX, NZ, ft, vocab), BF16)

    def place_a(ws, part, at):
        s, t = ws
        s = lax.dynamic_update_slice(s, part[:, None, :fs], (0, at, 0, 0))
        t = lax.dynamic_update_slice(t, part[:, None, fs:], (0, at, 0, 0))
        return s, t

    def place_b(ws, part, at):
        s, t = ws
        return s, lax.dynamic_update_slice(t, part[None], (at, 0, first, 0))

    ws = place_b(place_a((student_w, teacher_w), own_a, z), own_b, x)
    right_b = shifted(own_b, "x", NX, 1)
    left_b = shifted(own_b, "x", NX, -1)
    far_b = shifted(right_b, "x", NX, 1)
    right = left = own_a
    for step in range(1, NZ // 2 + 1):
        right = shifted(right, "z", NZ, 1)
        if step < NZ // 2:
            left = shifted(left, "z", NZ, -1)
        ws = place_a(ws, right, (z - step) % NZ)
        if step < NZ // 2:
            ws = place_a(ws, left, (z + step) % NZ)
        if step == 1:
            ws = place_b(place_b(ws, right_b, (x - 1) % NX), left_b, (x + 1) % NX)
        if step == 3:
            ws = place_b(ws, far_b, (x + 2) % NX)
    student_w = ws[0].reshape(NX * NZ * fs, vocab)
    teacher_w = ws[1].reshape(NC * NY, wide, vocab)

    student_normed = normalize(student_rows, student_gain)
    student_logits = jnp.dot(student_normed, student_w, preferred_element_type=F32)
    total = jnp.sum(rows[:, wide : wide + 3].astype(F32), axis=(0, 1))
    scale = lax.rsqrt(total / DT + epsilon)
    teacher_logits = (
        lax.dot_general(
            rows[:, :wide],
            teacher_w,
            (((0, 1), (0, 1)), ((), ())),
            preferred_element_type=F32,
        )
        * scale[:, None]
    )

    tops = [jnp.max(v, axis=1) for v in (teacher_logits, student_logits)]
    sums = [
        jnp.sum(jnp.exp(v - top[:, None]), axis=1)
        for v, top in zip((teacher_logits, student_logits), tops)
    ]
    stats = jnp.stack(tops + sums, axis=0)
    stats = jnp.broadcast_to(stats[None], (NC * NY,) + stats.shape)
    stats = lax.all_to_all(stats, ("core", "y"), 0, 0, tiled=True)
    top = jnp.max(stats[:, :2], axis=0)
    lse = top + jnp.log(jnp.sum(stats[:, 2:] * jnp.exp(stats[:, :2] - top), axis=0))
    live = (jnp.arange(tokens, dtype=jnp.int32) < lengths[0]).astype(F32)
    logit_grad = (
        live[:, None]
        * (jnp.exp(student_logits - lse[1][:, None]) - jnp.exp(teacher_logits - lse[0][:, None]))
    ).astype(BF16)

    half = tokens // NC

    def row_half(which):
        return lax.dot_general(
            lax.dynamic_slice_in_dim(logit_grad, which * half, half, 0),
            student_w,
            (((1,), (1,)), ((), ())),
            preferred_element_type=F32,
        )

    other = lax.ppermute(row_half(1 - c).astype(BF16), "core", [(0, 1), (1, 0)])
    mine = (row_half(c) + other.astype(F32)).astype(BF16)
    row_grad = lax.psum_scatter(mine, "y", scatter_dimension=0, tiled=True).astype(F32)

    head_part = lax.dot_general(
        student_normed, logit_grad, (((0,), (0,)), ((), ())), preferred_element_type=F32
    ).astype(BF16)
    head_part = lax.all_to_all(head_part.reshape(NX, NZ * fs, vocab), "x", 0, 0, tiled=True)
    head_part = jnp.sum(head_part.astype(F32), axis=0).astype(BF16)
    head_part = lax.all_to_all(head_part.reshape(NZ, fs, vocab), "z", 0, 0, tiled=True)
    head_grad = jnp.sum(head_part.astype(F32), axis=0)

    devices = NX * NZ * NC * NY
    squares = jnp.stack([jnp.sum(head_grad * head_grad), jnp.sum(row_grad * row_grad)])
    squares = jnp.broadcast_to(squares[None, :, None], (devices, 2, 64)).reshape(devices, 128)
    squares = lax.all_to_all(squares, ("x", "z", "core", "y"), 0, 0, tiled=True)
    squares = jnp.sum(squares, axis=0)
    head_update = head_grad * lax.rsqrt(squares[0] / (head_grad.size * devices) + epsilon)
    row_update = row_grad * lax.rsqrt(squares[64] / (row_grad.size * devices) + epsilon)
    return (head_update.astype(BF16).T, row_update.astype(BF16))


def solution(mesh):
    mesh = Mesh(mesh.devices.reshape(NX, NZ, NC, NY), ("x", "z", "core", "y"))
    dp, mp = ("x", "z"), ("core", "y")
    placed = (P(dp, mp), P(mp), P(mp, dp), P(dp, None), P(), P(mp, dp), P(dp))
    return jax.shard_map(
        body,
        mesh=mesh,
        in_specs=placed,
        out_specs=(P(mp, dp), P(dp + mp, None)),
        check_vma=False,
    )
```

```python
import jax
import jax.numpy as jnp
from jax import lax
from jax.experimental import pallas as pl
from jax.experimental.pallas import tpu as pltpu
from jax.sharding import Mesh, PartitionSpec as P

F32 = jnp.float32
BF16 = jnp.bfloat16
DT = 5120
NX, NZ, NC, NY = 4, 8, 2, 8
epsilon = 1e-06
HEAD_ROWS = 16
ANY = pl.BlockSpec(memory_space=pl.ANY)
VMEM = pl.BlockSpec(memory_space=pltpu.VMEM)
SMEM = pl.BlockSpec(memory_space=pltpu.SMEM)


def split3(values):
    high = values.astype(BF16)
    rest = values - high.astype(F32)
    middle = rest.astype(BF16)
    low = (rest - middle.astype(F32)).astype(BF16)
    return high, middle, low


def normalize(rows, gain):
    values = rows.astype(F32)
    mean_square = jnp.mean(values * values, axis=-1, keepdims=True)
    return (values * lax.rsqrt(mean_square + epsilon) * gain.astype(F32)).astype(BF16)


def shifted(values, axis, size, by):
    return lax.ppermute(values, axis, [(i, (i + by) % size) for i in range(size)])


def against(left, right, dims):
    return lax.dot_general(left, right, (dims, ((), ())), preferred_element_type=F32)


def logits_kernel(offsets, wide, fs, z_ref, rows_ref, *refs):
    blocks, refs = refs[: len(offsets)], refs[len(offsets) :]
    normed_ref, student_ref, teacher_ref, lse_ref, weights_ref = refs[:5]
    rows, squares, weights, row_sems, square_sem, student_sems, teacher_sems = refs[5:]
    z = z_ref[0]
    parts = rows_ref.shape[0]
    student_copies, teacher_copies, row_copies = [], [], []
    for k, (block, offset) in enumerate(zip(blocks, offsets)):
        at = lax.rem(z + offset + NZ, NZ)
        student_copies.append(
            pltpu.make_async_copy(
                block.at[:, pl.ds(0, fs)], weights_ref.at[:, at], student_sems.at[k]
            )
        )
        teacher_copies.append(
            pltpu.make_async_copy(
                block.at[:, pl.ds(fs, weights.shape[2])], weights.at[:, at], teacher_sems.at[k]
            )
        )
    for k in range(parts):
        row_copies.append(
            pltpu.make_async_copy(
                rows_ref.at[k, pl.ds(0, wide)], rows.at[pl.ds(k * wide, wide)], row_sems.at[k]
            )
        )
    square_copy = pltpu.make_async_copy(
        rows_ref.at[:, pl.ds(wide, HEAD_ROWS)], squares, square_sem
    )
    for copy in student_copies + teacher_copies + [square_copy] + row_copies:
        copy.start()

    vocab = weights.shape[3]
    for copy in student_copies:
        copy.wait()
    step = NZ * fs
    total = None
    for k in range(NX):
        part = against(
            weights_ref[k].reshape(step, vocab),
            normed_ref[pl.ds(k * step, step), :],
            ((0,), (0,)),
        )
        total = part if total is None else total + part
    student_ref[...] = total
    top = jnp.max(total, axis=0, keepdims=True)
    student_lse = top + jnp.log(jnp.sum(jnp.exp(total - top), axis=0, keepdims=True))

    for copy in teacher_copies:
        copy.wait()
    step = NZ * weights.shape[2]
    total = None
    for k in range(NX):
        for copy in row_copies[k * parts // NX : (k + 1) * parts // NX]:
            copy.wait()
        part = against(
            weights[k].reshape(step, vocab), rows[pl.ds(k * step, step), :], ((0,), (0,))
        )
        total = part if total is None else total + part
    square_copy.wait()
    square = jnp.sum(jnp.sum(squares[...].astype(F32), axis=0), axis=0, keepdims=True)
    total = total * lax.rsqrt(square / DT + epsilon)
    teacher_ref[...] = total
    top = jnp.max(total, axis=0, keepdims=True)
    teacher_lse = top + jnp.log(jnp.sum(jnp.exp(total - top), axis=0, keepdims=True))
    both = jnp.concatenate([teacher_lse, student_lse], axis=0)
    lse_ref[...] = jnp.broadcast_to(both[None], lse_ref.shape)


def logits(z, rows, blocks, offsets, normed, wide, fs):
    vocab = blocks[0].shape[2]
    ft = blocks[0].shape[1] - fs
    parts, _, tokens = rows.shape
    dma = pltpu.SemaphoreType.DMA
    flops = 2 * vocab * tokens * (parts * wide + normed.shape[0])

    def kernel(*refs):
        logits_kernel(offsets, wide, fs, *refs)

    return pl.pallas_call(
        kernel,
        out_shape=(
            jax.ShapeDtypeStruct((vocab, tokens), F32),
            jax.ShapeDtypeStruct((vocab, tokens), F32),
            jax.ShapeDtypeStruct((NC * NY, 2, tokens), F32),
            jax.ShapeDtypeStruct((NX, NZ, fs, vocab), BF16),
        ),
        in_specs=[SMEM, ANY] + [ANY] * len(blocks) + [VMEM],
        out_specs=(VMEM, VMEM, VMEM, VMEM),
        scratch_shapes=[
            pltpu.VMEM((parts * wide, tokens), BF16),
            pltpu.VMEM((parts, HEAD_ROWS, tokens), BF16),
            pltpu.VMEM((NX, NZ, ft, vocab), BF16),
            dma((parts,)),
            dma(()),
            dma((len(blocks),)),
            dma((len(blocks),)),
        ],
        compiler_params=pltpu.CompilerParams(vmem_limit_bytes=40 << 20),
        cost_estimate=pl.CostEstimate(
            flops=flops, bytes_accessed=20 << 20, transcendentals=2 * vocab * tokens
        ),
    )(z, rows, *blocks, normed)


def grad_kernel(
    which_ref, student_ref, teacher_ref, lse_ref, weights_ref, grad_ref, other_ref, mine_ref, turned
):
    tokens = student_ref.shape[1]
    lses = lse_ref[...]
    top = jnp.max(lses, axis=0)
    lse = top + jnp.log(jnp.sum(jnp.exp(lses - top[None]), axis=0))
    position = lax.broadcasted_iota(jnp.int32, (1, tokens), 1)
    live = (position < which_ref[1]).astype(F32)
    grad = live * (
        jnp.exp(student_ref[...] - lse[1:2]) - jnp.exp(teacher_ref[...] - lse[0:1])
    )
    grad_ref[...] = grad.astype(BF16)
    turned[...] = grad.T.astype(BF16)
    half = tokens // NC
    core = which_ref[0]
    mine = turned[pl.ds(pl.multiple_of(core * half, half), half), :]
    other = turned[pl.ds(pl.multiple_of((1 - core) * half, half), half), :]
    width = weights_ref.shape[0] // NX
    for k in range(NX):
        columns = pl.ds(k * width, width)
        block = weights_ref[columns, :]
        other_ref[:, columns] = against(other, block, ((1,), (1,))).astype(BF16)
        mine_ref[:, columns] = against(mine, block, ((1,), (1,)))


def gradient(which, student, teacher, lse, weights):
    vocab, tokens = student.shape
    features = weights.shape[0]
    half = tokens // NC
    return pl.pallas_call(
        grad_kernel,
        out_shape=(
            jax.ShapeDtypeStruct((vocab, tokens), BF16),
            jax.ShapeDtypeStruct((half, features), BF16),
            jax.ShapeDtypeStruct((half, features), F32),
        ),
        in_specs=[SMEM, VMEM, VMEM, VMEM, VMEM],
        out_specs=(VMEM, VMEM, VMEM),
        scratch_shapes=[pltpu.VMEM((tokens, vocab), BF16)],
        compiler_params=pltpu.CompilerParams(vmem_limit_bytes=40 << 20),
        cost_estimate=pl.CostEstimate(
            flops=2 * vocab * tokens * features,
            bytes_accessed=10 << 20,
            transcendentals=2 * vocab * tokens,
        ),
    )(which, student, teacher, lse, weights)


def body(
    teacher_rows, teacher_gain, teacher_head, student_rows, student_gain, student_head, lengths
):
    fs = student_head.shape[1]
    vocab = teacher_head.shape[0]
    z = lax.axis_index("z")
    c = lax.axis_index("core")

    heads = jnp.concatenate([student_head.T, teacher_head.T], axis=0)
    own = lax.all_gather(heads, "x", axis=0, tiled=False)
    blocks, offsets = [own], [0]
    right = left = own
    for step in range(1, NZ // 2 + 1):
        right = shifted(right, "z", NZ, 1)
        blocks.append(right)
        offsets.append(-step)
        if step < NZ // 2:
            left = shifted(left, "z", NZ, -1)
            blocks.append(left)
            offsets.append(step)

    teacher_rows, _ = lax.optimization_barrier((teacher_rows, own))
    block = teacher_rows.T
    wide = block.shape[0]
    values = block.astype(F32)
    scaled = (values * teacher_gain.astype(F32)[:, None]).astype(BF16)
    squares = jnp.stack(split3(jnp.sum(values * values, axis=0)), axis=0)
    sent = jnp.concatenate([scaled, jnp.pad(squares, ((0, HEAD_ROWS - 3), (0, 0)))], axis=0)
    rows = lax.all_gather(sent, ("core", "y"), axis=0, tiled=False)

    normed = normalize(student_rows, student_gain).T
    student_logits, teacher_logits, lse, student_w = logits(
        z[None], rows, blocks, offsets, normed, wide, fs
    )
    student_w = student_w.reshape(NX * NZ * fs, vocab)

    lse = lax.all_to_all(lse, ("core", "y"), 0, 0, tiled=True)
    which = jnp.stack([c, lengths[0]])
    logit_grad, other, mine = gradient(which, student_logits, teacher_logits, lse, student_w)

    other = lax.ppermute(other, "core", [(0, 1), (1, 0)])
    mine = (mine + other.astype(F32)).astype(BF16)
    row_grad = lax.psum_scatter(mine, "y", scatter_dimension=0, tiled=True).astype(F32)

    head_part = against(normed, logit_grad, ((1,), (1,))).astype(BF16)
    head_part = lax.all_to_all(head_part.reshape(NX, NZ * fs, vocab), "x", 0, 0, tiled=True)
    head_part = jnp.sum(head_part.astype(F32), axis=0).astype(BF16)
    head_part = lax.all_to_all(head_part.reshape(NZ, fs, vocab), "z", 0, 0, tiled=True)
    head_grad = jnp.sum(head_part.astype(F32), axis=0)

    devices = NX * NZ * NC * NY
    squares = jnp.stack([jnp.sum(head_grad * head_grad), jnp.sum(row_grad * row_grad)])
    squares = jnp.broadcast_to(squares[None, :, None], (devices, 2, 64)).reshape(devices, 128)
    squares = lax.all_to_all(squares, ("x", "z", "core", "y"), 0, 0, tiled=True)
    squares = jnp.sum(squares, axis=0)
    head_update = head_grad * lax.rsqrt(squares[0] / (head_grad.size * devices) + epsilon)
    row_update = row_grad * lax.rsqrt(squares[64] / (row_grad.size * devices) + epsilon)
    return (head_update.astype(BF16).T, row_update.astype(BF16))


def solution(mesh):
    mesh = Mesh(mesh.devices.reshape(NX, NZ, NC, NY), ("x", "z", "core", "y"))
    dp, mp = ("x", "z"), ("core", "y")
    placed = (P(dp, mp), P(mp), P(mp, dp), P(dp, None), P(), P(mp, dp), P(dp))
    return jax.shard_map(
        body,
        mesh=mesh,
        in_specs=placed,
        out_specs=(P(mp, dp), P(dp + mp, None)),
        check_vma=False,
    )
```

```python
import jax
import jax.numpy as jnp
from jax import lax
from jax.experimental import pallas as pl
from jax.experimental.pallas import tpu as pltpu
from jax.sharding import Mesh, PartitionSpec as P

F32 = jnp.float32
BF16 = jnp.bfloat16
DT = 5120
NX, NZ, NC, NY = 4, 8, 2, 8
epsilon = 1e-06
HEAD_ROWS = 16
HBM = pl.BlockSpec(memory_space=pltpu.HBM)
VMEM = pl.BlockSpec(memory_space=pltpu.VMEM)
SMEM = pl.BlockSpec(memory_space=pltpu.SMEM)


def split3(values):
    high = values.astype(BF16)
    rest = values - high.astype(F32)
    middle = rest.astype(BF16)
    low = (rest - middle.astype(F32)).astype(BF16)
    return high, middle, low


def normalize(rows, gain):
    values = rows.astype(F32)
    mean_square = jnp.mean(values * values, axis=-1, keepdims=True)
    return (values * lax.rsqrt(mean_square + epsilon) * gain.astype(F32)).astype(BF16)


def shifted(values, axis, size, by):
    return lax.ppermute(values, axis, [(i, (i + by) % size) for i in range(size)])


def against(left, right, dims):
    return lax.dot_general(left, right, (dims, ((), ())), preferred_element_type=F32)


def log_sum_exp(values):
    top = jnp.max(values, axis=0, keepdims=True)
    return top + jnp.log(jnp.sum(jnp.exp(values - top), axis=0, keepdims=True))


def begin(copies):
    for copy in copies:
        copy.start()
    return copies


def finish(copies):
    for copy in copies:
        copy.wait()


def most_kernel(offsets, missing, wide, fs, z_ref, rows_ref, normed_ref, *refs):
    blocks, refs = refs[: len(offsets)], refs[len(offsets) :]
    student_ref, teacher_ref, scale_ref, weights_ref, last_rows, last_normed = refs[:6]
    rows, squares, student_w, teacher_w, normed = refs[6:11]
    row_sems, square_sem, student_sems, teacher_sems, normed_sem, weights_sem, last_sems = refs[11:]
    z = z_ref[0]
    parts = rows_ref.shape[0]
    ft, vocab = teacher_w.shape[2:]
    places = [lax.rem(z + offset + NZ, NZ) for offset in offsets]
    student_copies = [
        pltpu.make_async_copy(
            block.at[:, pl.ds(0, fs)], student_w.at[:, at], student_sems.at[k]
        )
        for k, (block, at) in enumerate(zip(blocks, places))
    ]
    normed_copy = pltpu.make_async_copy(normed_ref, normed, normed_sem)
    teacher_copies = [
        pltpu.make_async_copy(
            block.at[:, pl.ds(fs, ft)], teacher_w.at[:, at], teacher_sems.at[k]
        )
        for k, (block, at) in enumerate(zip(blocks, places))
    ]
    square_copy = pltpu.make_async_copy(
        rows_ref.at[:, pl.ds(wide, HEAD_ROWS)], squares, square_sem
    )
    row_copies = [
        pltpu.make_async_copy(
            rows_ref.at[k, pl.ds(0, wide)], rows.at[pl.ds(k * wide, wide)], row_sems.at[k]
        )
        for k in range(parts)
    ]
    at = lax.rem(z + missing + NZ, NZ)
    per_block = parts // NX
    fold = NZ // per_block
    inner = pl.multiple_of(lax.rem(at, fold) * ft, 16)
    last_copies = []
    for k in range(NX):
        source = pl.multiple_of(k * NZ * fs + at * fs, 16)
        last_copies.append(
            pltpu.make_async_copy(
                normed_ref.at[pl.ds(source, fs)],
                last_normed.at[pl.ds(k * fs, fs)],
                last_sems.at[k],
            )
        )
        last_copies.append(
            pltpu.make_async_copy(
                rows_ref.at[k * per_block + lax.div(at, fold), pl.ds(inner, ft)],
                last_rows.at[pl.ds(k * ft, ft)],
                last_sems.at[NX + k],
            )
        )
    begin(student_copies + [normed_copy] + teacher_copies + [square_copy] + row_copies)
    begin(last_copies)
    student_w[:, at] = jnp.zeros((NX, fs, vocab), BF16)
    teacher_w[:, at] = jnp.zeros((NX, ft, vocab), BF16)

    finish(student_copies + [normed_copy])
    weights_copy = pltpu.make_async_copy(student_w, weights_ref, weights_sem)
    weights_copy.start()
    step = NZ * fs
    total = None
    for k in range(NX):
        part = against(
            student_w[k].reshape(step, vocab), normed[pl.ds(k * step, step), :], ((0,), (0,))
        )
        total = part if total is None else total + part
    student_ref[...] = total

    finish(teacher_copies)
    step = NZ * ft
    total = None
    for k in range(NX):
        finish(row_copies[k * parts // NX : (k + 1) * parts // NX])
        part = against(
            teacher_w[k].reshape(step, vocab), rows[pl.ds(k * step, step), :], ((0,), (0,))
        )
        total = part if total is None else total + part
    teacher_ref[...] = total
    square_copy.wait()
    square = jnp.sum(jnp.sum(squares[...].astype(F32), axis=0), axis=0, keepdims=True)
    scale_ref[...] = lax.rsqrt(square / DT + epsilon)
    finish(last_copies + [weights_copy])


def most(z, rows, normed, blocks, offsets, missing, wide, fs):
    vocab = blocks[0].shape[2]
    ft = blocks[0].shape[1] - fs
    parts, _, tokens = rows.shape
    dma = pltpu.SemaphoreType.DMA

    def kernel(*refs):
        most_kernel(offsets, missing, wide, fs, *refs)

    return pl.pallas_call(
        kernel,
        out_shape=(
            jax.ShapeDtypeStruct((vocab, tokens), F32),
            jax.ShapeDtypeStruct((vocab, tokens), F32),
            jax.ShapeDtypeStruct((1, tokens), F32),
            jax.ShapeDtypeStruct((NX, NZ, fs, vocab), BF16),
            jax.ShapeDtypeStruct((NX * ft, tokens), BF16),
            jax.ShapeDtypeStruct((NX * fs, tokens), BF16),
        ),
        in_specs=[SMEM, HBM, HBM] + [HBM] * len(blocks),
        out_specs=(VMEM, VMEM, VMEM, HBM, VMEM, VMEM),
        scratch_shapes=[
            pltpu.VMEM((parts * wide, tokens), BF16),
            pltpu.VMEM((parts, HEAD_ROWS, tokens), BF16),
            pltpu.VMEM((NX, NZ, fs, vocab), BF16),
            pltpu.VMEM((NX, NZ, ft, vocab), BF16),
            pltpu.VMEM(normed.shape, BF16),
            dma((parts,)),
            dma(()),
            dma((len(blocks),)),
            dma((len(blocks),)),
            dma(()),
            dma(()),
            dma((2 * NX,)),
        ],
        compiler_params=pltpu.CompilerParams(vmem_limit_bytes=32 << 20),
        cost_estimate=pl.CostEstimate(
            flops=2 * vocab * tokens * (parts * wide + normed.shape[0]),
            bytes_accessed=20 << 20,
            transcendentals=0,
        ),
    )(z, rows, normed, *blocks)


def last_kernel(missing, fs, z_ref, rows_ref, normed_ref, block_ref, *refs):
    student_part, teacher_part, scale_ref, _, student_ref, teacher_ref, lse_ref, weights_ref = refs[:8]
    student_w, teacher_w, sems = refs[8:]
    ft, vocab = teacher_w.shape[1:]
    at = lax.rem(z_ref[0] + missing + NZ, NZ)
    copies = begin(
        [
            pltpu.make_async_copy(block_ref.at[:, pl.ds(0, fs)], student_w, sems.at[0]),
            pltpu.make_async_copy(block_ref.at[:, pl.ds(fs, ft)], teacher_w, sems.at[1]),
        ]
    )
    copies[0].wait()
    weights_copy = pltpu.make_async_copy(student_w, weights_ref.at[:, at], sems.at[2])
    weights_copy.start()
    total = student_part[...] + against(
        student_w[...].reshape(NX * fs, vocab), normed_ref[...], ((0,), (0,))
    )
    student_ref[...] = total
    student_lse = log_sum_exp(total)
    copies[1].wait()
    total = scale_ref[...] * (
        teacher_part[...]
        + against(teacher_w[...].reshape(NX * ft, vocab), rows_ref[...], ((0,), (0,)))
    )
    teacher_ref[...] = total
    both = jnp.concatenate([log_sum_exp(total), student_lse], axis=0)
    lse_ref[...] = jnp.broadcast_to(both[None], lse_ref.shape)
    weights_copy.wait()


def last(z, rows, normed, block, student, teacher, scale, weights, missing, fs):
    vocab, tokens = student.shape
    ft = block.shape[1] - fs

    def kernel(*refs):
        last_kernel(missing, fs, *refs)

    return pl.pallas_call(
        kernel,
        out_shape=(
            jax.ShapeDtypeStruct((vocab, tokens), F32),
            jax.ShapeDtypeStruct((vocab, tokens), F32),
            jax.ShapeDtypeStruct((NC * NY, 2, tokens), F32),
            jax.ShapeDtypeStruct(weights.shape, BF16),
        ),
        in_specs=[SMEM, VMEM, VMEM, HBM, VMEM, VMEM, VMEM, HBM],
        out_specs=(VMEM, VMEM, VMEM, HBM),
        input_output_aliases={7: 3},
        scratch_shapes=[
            pltpu.VMEM((NX, fs, vocab), BF16),
            pltpu.VMEM((NX, ft, vocab), BF16),
            pltpu.SemaphoreType.DMA((3,)),
        ],
        compiler_params=pltpu.CompilerParams(vmem_limit_bytes=24 << 20),
        cost_estimate=pl.CostEstimate(
            flops=2 * vocab * tokens * NX * (ft + fs),
            bytes_accessed=8 << 20,
            transcendentals=2 * vocab * tokens,
        ),
    )(z, rows, normed, block, student, teacher, scale, weights)


def grad_kernel(which_ref, student, teacher, lse_ref, weights, *refs):
    grad_ref, other_ref, mine_ref, turned = refs
    tokens = student.shape[1]
    lses = lse_ref[...]
    top = jnp.max(lses, axis=0)
    lse = top + jnp.log(jnp.sum(jnp.exp(lses - top[None]), axis=0))
    position = lax.broadcasted_iota(jnp.int32, (1, tokens), 1)
    live = (position < which_ref[1]).astype(F32)
    grad = live * (jnp.exp(student[...] - lse[1:2]) - jnp.exp(teacher[...] - lse[0:1]))
    grad_ref[...] = grad.astype(BF16)
    turned[...] = grad.T.astype(BF16)
    half = tokens // NC
    core = which_ref[0]
    mine = turned[pl.ds(pl.multiple_of(core * half, half), half), :]
    other = turned[pl.ds(pl.multiple_of((1 - core) * half, half), half), :]
    width = weights.shape[0] // NX
    for k in range(NX):
        columns = pl.ds(k * width, width)
        block = weights[columns, :]
        other_ref[:, columns] = against(other, block, ((1,), (1,))).astype(BF16)
        mine_ref[:, columns] = against(mine, block, ((1,), (1,)))


def gradient(which, student, teacher, lse, weights):
    vocab, tokens = student.shape
    features = weights.shape[0]
    half = tokens // NC
    return pl.pallas_call(
        grad_kernel,
        out_shape=(
            jax.ShapeDtypeStruct((vocab, tokens), BF16),
            jax.ShapeDtypeStruct((half, features), BF16),
            jax.ShapeDtypeStruct((half, features), F32),
        ),
        in_specs=[SMEM, VMEM, VMEM, VMEM, VMEM],
        out_specs=(VMEM, VMEM, VMEM),
        scratch_shapes=[pltpu.VMEM((tokens, vocab), BF16)],
        compiler_params=pltpu.CompilerParams(vmem_limit_bytes=24 << 20),
        cost_estimate=pl.CostEstimate(
            flops=2 * vocab * tokens * features,
            bytes_accessed=10 << 20,
            transcendentals=2 * vocab * tokens,
        ),
    )(which, student, teacher, lse, weights)


def head_kernel(normed_hbm, grad_ref, out_ref, normed, sems):
    width = normed.shape[0] // NX
    rows = [pl.ds(k * width, width) for k in range(NX)]
    copies = begin(
        [
            pltpu.make_async_copy(normed_hbm.at[rows[k]], normed.at[rows[k]], sems.at[k])
            for k in range(NX)
        ]
    )
    for k in range(NX):
        copies[k].wait()
        out_ref[rows[k], :] = against(normed[rows[k], :], grad_ref[...], ((1,), (1,))).astype(BF16)


def head_product(normed, grad):
    features, tokens = normed.shape
    vocab = grad.shape[0]
    return pl.pallas_call(
        head_kernel,
        out_shape=jax.ShapeDtypeStruct((features, vocab), BF16),
        in_specs=[HBM, VMEM],
        out_specs=VMEM,
        scratch_shapes=[pltpu.VMEM(normed.shape, BF16), pltpu.SemaphoreType.DMA((NX,))],
        compiler_params=pltpu.CompilerParams(vmem_limit_bytes=16 << 20),
        cost_estimate=pl.CostEstimate(
            flops=2 * vocab * tokens * features, bytes_accessed=5 << 20, transcendentals=0
        ),
    )(normed, grad)


def squares_kernel(parts_ref, row_ref, head_ref, out_ref):
    head = jnp.sum(parts_ref[...].astype(F32), axis=0)
    head_ref[...] = head
    row = row_ref[...].astype(F32)
    lane = lax.broadcasted_iota(jnp.int32, out_ref.shape, 1)
    out_ref[...] = jnp.where(lane < 64, jnp.sum(head * head), jnp.sum(row * row))


def updates_kernel(devices, squares_ref, head_ref, row_ref, head_out, row_out):
    squares = jnp.sum(squares_ref[...], axis=0, keepdims=True)
    head = head_ref[...]
    row = row_ref[...].astype(F32)
    head_out[...] = (
        head * lax.rsqrt(squares[:, :1] / (head.size * devices) + epsilon)
    ).astype(BF16)
    row_out[...] = (
        row * lax.rsqrt(squares[:, 64:65] / (row.size * devices) + epsilon)
    ).astype(BF16)


def body(
    teacher_rows, teacher_gain, teacher_head, student_rows, student_gain, student_head, lengths
):
    fs = student_head.shape[1]
    vocab = teacher_head.shape[0]
    z = lax.axis_index("z")
    c = lax.axis_index("core")

    heads = jnp.concatenate([student_head.T, teacher_head.T], axis=0)
    own = lax.all_gather(heads, "x", axis=0, tiled=False)
    blocks, offsets = [own], [0]
    right = left = own
    for step in range(1, NZ // 2 + 1):
        right = shifted(right, "z", NZ, 1)
        blocks.append(right)
        offsets.append(-step)
        if step < NZ // 2:
            left = shifted(left, "z", NZ, -1)
            blocks.append(left)
            offsets.append(step)

    teacher_rows, _ = lax.optimization_barrier((teacher_rows, own))
    block = teacher_rows.T
    wide = block.shape[0]
    values = block.astype(F32)
    scaled = (values * teacher_gain.astype(F32)[:, None]).astype(BF16)
    squares = jnp.stack(split3(jnp.sum(values * values, axis=0)), axis=0)
    sent = jnp.concatenate([scaled, jnp.pad(squares, ((0, HEAD_ROWS - 3), (0, 0)))], axis=0)
    rows = lax.all_gather(sent, ("core", "y"), axis=0, tiled=False)

    normed = normalize(student_rows, student_gain).T
    missing = offsets[-1]
    student_logits, teacher_logits, scale, weights, last_rows, last_normed = most(
        z[None], rows, normed, blocks[:-1], offsets[:-1], missing, wide, fs
    )
    student_logits, teacher_logits, lse, weights = last(
        z[None],
        last_rows,
        last_normed,
        blocks[-1],
        student_logits,
        teacher_logits,
        scale,
        weights,
        missing,
        fs,
    )
    student_w = weights.reshape(NX * NZ * fs, vocab)

    lse = lax.all_to_all(lse, ("core", "y"), 0, 0, tiled=True)
    which = jnp.stack([c, lengths[0]])
    logit_grad, other, mine = gradient(which, student_logits, teacher_logits, lse, student_w)

    other = lax.ppermute(other, "core", [(0, 1), (1, 0)])
    head_part = head_product(normed, logit_grad)
    other, head_part = lax.optimization_barrier((other, head_part))
    mine = (mine + other.astype(F32)).astype(BF16)
    row_grad = lax.psum_scatter(mine, "y", scatter_dimension=0, tiled=True)

    head_part = lax.all_to_all(head_part.reshape(NX, NZ * fs, vocab), "x", 0, 0, tiled=True)
    head_part = jnp.sum(head_part.astype(F32), axis=0).astype(BF16)
    head_part = lax.all_to_all(head_part.reshape(NZ, fs, vocab), "z", 0, 0, tiled=True)

    devices = NX * NZ * NC * NY
    head_grad, squares = pl.pallas_call(
        squares_kernel,
        out_shape=(
            jax.ShapeDtypeStruct((fs, vocab), F32),
            jax.ShapeDtypeStruct((devices, 128), F32),
        ),
    )(head_part, row_grad)
    squares = lax.all_to_all(squares, ("x", "z", "core", "y"), 0, 0, tiled=True)
    head_update, row_update = pl.pallas_call(
        lambda *refs: updates_kernel(devices, *refs),
        out_shape=(
            jax.ShapeDtypeStruct((fs, vocab), BF16),
            jax.ShapeDtypeStruct(row_grad.shape, BF16),
        ),
    )(squares, head_grad, row_grad)
    return (head_update.T, row_update)


def solution(mesh):
    mesh = Mesh(mesh.devices.reshape(NX, NZ, NC, NY), ("x", "z", "core", "y"))
    dp, mp = ("x", "z"), ("core", "y")
    placed = (P(dp, mp), P(mp), P(mp, dp), P(dp, None), P(), P(mp, dp), P(dp))
    return jax.shard_map(
        body,
        mesh=mesh,
        in_specs=placed,
        out_specs=(P(mp, dp), P(dp + mp, None)),
        check_vma=False,
    )
```

```python
import jax
import jax.numpy as jnp
from jax import lax
from jax.experimental import pallas as pl
from jax.experimental.pallas import tpu as pltpu
from jax.sharding import Mesh, PartitionSpec as P

F32 = jnp.float32
BF16 = jnp.bfloat16
DT = 5120
NX, NZ, NC, NY = 4, 8, 2, 8
epsilon = 1e-06
HEAD_ROWS = 16
LSE_ROWS = 8
GRANT = 60 << 20
HBM = pl.BlockSpec(memory_space=pltpu.HBM)
VMEM = pl.BlockSpec(memory_space=pltpu.VMEM)
SMEM = pl.BlockSpec(memory_space=pltpu.SMEM)


def split3(values):
    high = values.astype(BF16)
    rest = values - high.astype(F32)
    middle = rest.astype(BF16)
    low = (rest - middle.astype(F32)).astype(BF16)
    return high, middle, low


def normalize(rows, gain):
    values = rows.astype(F32)
    mean_square = jnp.mean(values * values, axis=-1, keepdims=True)
    return (values * lax.rsqrt(mean_square + epsilon) * gain.astype(F32)).astype(BF16)


def along(values):
    pairs = [(i * NC + c, (i + 1 - 2 * c) % NZ * NC + c) for i in range(NZ) for c in range(NC)]
    return lax.ppermute(values, ("z", "core"), pairs)


def swapped(values):
    return lax.ppermute(values, "core", [(0, 1), (1, 0)])


def against(left, right, dims):
    return lax.dot_general(left, right, (dims, ((), ())), preferred_element_type=F32)


def log_sum_exp(values):
    top = jnp.max(values, axis=0, keepdims=True)
    return top + jnp.log(jnp.sum(jnp.exp(values - top), axis=0, keepdims=True))


def place_of(where_ref, offset):
    return lax.rem(where_ref[0] + where_ref[1] * offset + NZ, NZ)


def begin(copies):
    for copy in copies:
        copy.start()
    return copies


def finish(copies):
    for copy in copies:
        copy.wait()


def most_kernel(offsets, missing, wide, fs, where_ref, rows_ref, normed_ref, *refs):
    blocks, refs = refs[: len(offsets)], refs[len(offsets) :]
    student_ref, teacher_ref, scale_ref, weights_ref = refs[:4]
    rows, squares, student_w, teacher_w, normed, student, teacher = refs[4:11]
    row_sems, square_sem, student_sems, teacher_sems, normed_sem, out_sems = refs[11:]
    parts = rows_ref.shape[0]
    ft, vocab = teacher_w.shape[2:]
    places = [place_of(where_ref, offset) for offset in offsets]
    student_copies = [
        pltpu.make_async_copy(
            block.at[:, pl.ds(0, fs)], student_w.at[:, at], student_sems.at[k]
        )
        for k, (block, at) in enumerate(zip(blocks, places))
    ]
    normed_copy = pltpu.make_async_copy(normed_ref, normed, normed_sem)
    teacher_copies = [
        pltpu.make_async_copy(
            block.at[:, pl.ds(fs, ft)], teacher_w.at[:, at], teacher_sems.at[k]
        )
        for k, (block, at) in enumerate(zip(blocks, places))
    ]
    square_copy = pltpu.make_async_copy(
        rows_ref.at[:, pl.ds(wide, HEAD_ROWS)], squares, square_sem
    )
    row_copies = [
        pltpu.make_async_copy(
            rows_ref.at[k, pl.ds(0, wide)], rows.at[pl.ds(k * wide, wide)], row_sems.at[k]
        )
        for k in range(parts)
    ]
    absent = [place_of(where_ref, offset) for offset in missing]
    begin(student_copies + [normed_copy] + teacher_copies + [square_copy] + row_copies)
    for at in absent:
        student_w[:, at] = jnp.zeros((NX, fs, vocab), BF16)
        teacher_w[:, at] = jnp.zeros((NX, ft, vocab), BF16)

    finish(student_copies + [normed_copy])
    out_copies = [
        pltpu.make_async_copy(source, out, out_sems.at[k])
        for k, (source, out) in enumerate(
            [(student_w, weights_ref), (student, student_ref), (teacher, teacher_ref)]
        )
    ]
    out_copies[0].start()
    step = NZ * fs
    total = None
    for k in range(NX):
        part = against(
            student_w[k].reshape(step, vocab), normed[pl.ds(k * step, step), :], ((0,), (0,))
        )
        total = part if total is None else total + part
    student[...] = total
    out_copies[1].start()

    finish(teacher_copies)
    step = NZ * ft
    total = None
    for k in range(NX):
        finish(row_copies[k * parts // NX : (k + 1) * parts // NX])
        part = against(
            teacher_w[k].reshape(step, vocab), rows[pl.ds(k * step, step), :], ((0,), (0,))
        )
        total = part if total is None else total + part
    teacher[...] = total
    out_copies[2].start()
    square_copy.wait()
    square = jnp.sum(jnp.sum(squares[...].astype(F32), axis=0), axis=0, keepdims=True)
    scale_ref[...] = lax.rsqrt(square / DT + epsilon)
    finish(out_copies)


def most(where, rows, normed, blocks, offsets, missing, wide, fs):
    vocab = blocks[0].shape[2]
    ft = blocks[0].shape[1] - fs
    parts, _, tokens = rows.shape
    dma = pltpu.SemaphoreType.DMA

    def kernel(*refs):
        most_kernel(offsets, missing, wide, fs, *refs)

    return pl.pallas_call(
        kernel,
        out_shape=(
            jax.ShapeDtypeStruct((vocab, tokens), F32),
            jax.ShapeDtypeStruct((vocab, tokens), F32),
            jax.ShapeDtypeStruct((1, tokens), F32),
            jax.ShapeDtypeStruct((NX, NZ, fs, vocab), BF16),
        ),
        in_specs=[SMEM, HBM, HBM] + [HBM] * len(blocks),
        out_specs=(HBM, HBM, VMEM, HBM),
        scratch_shapes=[
            pltpu.VMEM((parts * wide, tokens), BF16),
            pltpu.VMEM((parts, HEAD_ROWS, tokens), BF16),
            pltpu.VMEM((NX, NZ, fs, vocab), BF16),
            pltpu.VMEM((NX, NZ, ft, vocab), BF16),
            pltpu.VMEM(normed.shape, BF16),
            pltpu.VMEM((vocab, tokens), F32),
            pltpu.VMEM((vocab, tokens), F32),
            dma((parts,)),
            dma(()),
            dma((len(blocks),)),
            dma((len(blocks),)),
            dma(()),
            dma((3,)),
        ],
        compiler_params=pltpu.CompilerParams(vmem_limit_bytes=GRANT),
        cost_estimate=pl.CostEstimate(
            flops=2 * vocab * tokens * (parts * wide + normed.shape[0]),
            bytes_accessed=20 << 20,
            transcendentals=0,
        ),
    )(where, rows, normed, *blocks)


def last_kernel(missing, fs, where_ref, rows_ref, normed_ref, student_part, teacher_part, *refs):
    scale_ref, _, *blocks = refs[: 2 + len(missing)]
    student_ref, teacher_ref, lse_ref, weights_ref = refs[2 + len(missing) : 6 + len(missing)]
    rows, normed, student_w, teacher_w, student, teacher, sems, out_sems = refs[6 + len(missing) :]
    ft, vocab = teacher_w.shape[2:]
    per_block = rows_ref.shape[0] // NX
    fold = NZ // per_block
    places = [place_of(where_ref, offset) for offset in missing]
    first = [pltpu.make_async_copy(student_part, student, sems.at[0, 0])]
    second = [pltpu.make_async_copy(teacher_part, teacher, sems.at[0, 1])]
    for i, (block, at) in enumerate(zip(blocks, places)):
        copy_sems = sems.at[1 + i]
        inner = pl.multiple_of(lax.rem(at, fold) * ft, 16)
        first.append(
            pltpu.make_async_copy(block.at[:, pl.ds(0, fs)], student_w.at[i], copy_sems.at[0])
        )
        second.append(
            pltpu.make_async_copy(block.at[:, pl.ds(fs, ft)], teacher_w.at[i], copy_sems.at[1])
        )
        for k in range(NX):
            source = pl.multiple_of(k * NZ * fs + at * fs, 16)
            first.append(
                pltpu.make_async_copy(
                    normed_ref.at[pl.ds(source, fs)],
                    normed.at[i, pl.ds(k * fs, fs)],
                    copy_sems.at[2 + k],
                )
            )
            second.append(
                pltpu.make_async_copy(
                    rows_ref.at[k * per_block + lax.div(at, fold), pl.ds(inner, ft)],
                    rows.at[i, pl.ds(k * ft, ft)],
                    copy_sems.at[2 + NX + k],
                )
            )
    begin(first + second)
    finish(first)
    out_copies = [
        pltpu.make_async_copy(student_w.at[i], weights_ref.at[:, at], out_sems.at[2 + i])
        for i, at in enumerate(places)
    ]
    begin(out_copies)
    total = student[...]
    for i in range(len(missing)):
        total += against(student_w[i].reshape(NX * fs, vocab), normed[i], ((0,), (0,)))
    student[...] = total
    out_copies.append(pltpu.make_async_copy(student, student_ref, out_sems.at[0]))
    out_copies[-1].start()
    student_lse = log_sum_exp(total)
    finish(second)
    total = teacher[...]
    for i in range(len(missing)):
        total += against(teacher_w[i].reshape(NX * ft, vocab), rows[i], ((0,), (0,)))
    total = scale_ref[...] * total
    teacher[...] = total
    out_copies.append(pltpu.make_async_copy(teacher, teacher_ref, out_sems.at[1]))
    out_copies[-1].start()
    both = jnp.concatenate([log_sum_exp(total), student_lse], axis=0)
    both = jnp.concatenate([both] * (lse_ref.shape[1] // 2), axis=0)
    lse_ref[...] = jnp.broadcast_to(both[None], lse_ref.shape)
    finish(out_copies)


def last(where, rows, normed, blocks, student, teacher, scale, weights, missing, fs):
    vocab, tokens = student.shape
    ft = blocks[0].shape[1] - fs
    count = len(blocks)

    def kernel(*refs):
        last_kernel(missing, fs, *refs)

    return pl.pallas_call(
        kernel,
        out_shape=(
            jax.ShapeDtypeStruct((vocab, tokens), F32),
            jax.ShapeDtypeStruct((vocab, tokens), F32),
            jax.ShapeDtypeStruct((NC * NY, LSE_ROWS, tokens), F32),
            jax.ShapeDtypeStruct(weights.shape, BF16),
        ),
        in_specs=[SMEM, HBM, HBM, HBM, HBM, VMEM] + [HBM] * (1 + count),
        out_specs=(HBM, HBM, VMEM, HBM),
        input_output_aliases={6: 3},
        scratch_shapes=[
            pltpu.VMEM((count, NX * ft, tokens), BF16),
            pltpu.VMEM((count, NX * fs, tokens), BF16),
            pltpu.VMEM((count, NX, fs, vocab), BF16),
            pltpu.VMEM((count, NX, ft, vocab), BF16),
            pltpu.VMEM((vocab, tokens), F32),
            pltpu.VMEM((vocab, tokens), F32),
            pltpu.SemaphoreType.DMA((1 + count, 2 + 2 * NX)),
            pltpu.SemaphoreType.DMA((2 + count,)),
        ],
        compiler_params=pltpu.CompilerParams(vmem_limit_bytes=GRANT),
        cost_estimate=pl.CostEstimate(
            flops=2 * vocab * tokens * NX * (ft + fs) * count,
            bytes_accessed=8 << 20,
            transcendentals=2 * vocab * tokens,
        ),
    )(where, rows, normed, student, teacher, scale, weights, *blocks)


def grad_kernel(which_ref, student_hbm, teacher_hbm, lse_ref, weights_hbm, normed_hbm, *refs):
    other_hbm, mine_hbm, head_hbm = refs[:3]
    student, teacher, weights, normed, grad_t, turned, other, mine, head, sems, out_sems = refs[3:]
    copies = begin(
        [
            pltpu.make_async_copy(source, held, sems.at[k])
            for k, (source, held) in enumerate(
                [
                    (student_hbm, student),
                    (teacher_hbm, teacher),
                    (weights_hbm, weights),
                    (normed_hbm, normed),
                ]
            )
        ]
    )
    tokens = student.shape[1]
    lses = lse_ref[:, 0:2]
    top = jnp.max(lses, axis=0)
    lse = top + jnp.log(jnp.sum(jnp.exp(lses - top[None]), axis=0))
    position = lax.broadcasted_iota(jnp.int32, (1, tokens), 1)
    live = (position < which_ref[1]).astype(F32)
    finish(copies[:2])
    grad = live * (jnp.exp(student[...] - lse[1:2]) - jnp.exp(teacher[...] - lse[0:1]))
    grad_t[...] = grad.astype(BF16)
    turned[...] = grad.T.astype(BF16)
    half = tokens // NC
    core = which_ref[0]
    parts = [
        (other, other_hbm, turned[pl.ds(pl.multiple_of((1 - core) * half, half), half), :]),
        (mine, mine_hbm, turned[pl.ds(pl.multiple_of(core * half, half), half), :]),
    ]
    width = weights.shape[0] // NX
    slices = [pl.ds(k * width, width) for k in range(NX)]
    copies[2].wait()
    out_copies = []
    for i, (out, hbm, block) in enumerate(parts):
        for columns in slices:
            out[:, columns] = against(block, weights[columns, :], ((1,), (1,))).astype(BF16)
        out_copies.append(pltpu.make_async_copy(out, hbm, out_sems.at[i]))
        out_copies[-1].start()
    copies[3].wait()
    for k, rows in enumerate(slices):
        head[rows, :] = against(normed[rows, :], grad_t[...], ((1,), (1,))).astype(BF16)
        out_copies.append(pltpu.make_async_copy(head.at[rows], head_hbm.at[rows], out_sems.at[2 + k]))
        out_copies[-1].start()
    finish(out_copies)


def gradient(which, student, teacher, lse, weights, normed):
    vocab, tokens = student.shape
    features = weights.shape[0]
    half = tokens // NC
    return pl.pallas_call(
        grad_kernel,
        out_shape=(
            jax.ShapeDtypeStruct((half, features), BF16),
            jax.ShapeDtypeStruct((half, features), BF16),
            jax.ShapeDtypeStruct((features, vocab), BF16),
        ),
        in_specs=[SMEM, HBM, HBM, VMEM, HBM, HBM],
        out_specs=(HBM, HBM, HBM),
        scratch_shapes=[
            pltpu.VMEM((vocab, tokens), F32),
            pltpu.VMEM((vocab, tokens), F32),
            pltpu.VMEM((features, vocab), BF16),
            pltpu.VMEM((features, tokens), BF16),
            pltpu.VMEM((vocab, tokens), BF16),
            pltpu.VMEM((tokens, vocab), BF16),
            pltpu.VMEM((half, features), BF16),
            pltpu.VMEM((half, features), BF16),
            pltpu.VMEM((features, vocab), BF16),
            pltpu.SemaphoreType.DMA((4,)),
            pltpu.SemaphoreType.DMA((2 + NX,)),
        ],
        compiler_params=pltpu.CompilerParams(vmem_limit_bytes=GRANT),
        cost_estimate=pl.CostEstimate(
            flops=4 * vocab * tokens * features,
            bytes_accessed=10 << 20,
            transcendentals=2 * vocab * tokens,
        ),
    )(which, student, teacher, lse, weights, normed)


def squares_kernel(parts_ref, row_ref, head_ref, out_ref):
    head = jnp.sum(parts_ref[...].astype(F32), axis=0)
    head_ref[...] = head
    row = row_ref[...].astype(F32)
    lane = lax.broadcasted_iota(jnp.int32, out_ref.shape, 1)
    out_ref[...] = jnp.where(lane < 64, jnp.sum(head * head), jnp.sum(row * row))


def updates_kernel(devices, squares_ref, head_ref, row_ref, head_out, row_out):
    squares = jnp.sum(squares_ref[...], axis=0, keepdims=True)
    head = head_ref[...]
    row = row_ref[...].astype(F32)
    head_out[...] = (
        head * lax.rsqrt(squares[:, :1] / (head.size * devices) + epsilon)
    ).astype(BF16)
    row_out[...] = (
        row * lax.rsqrt(squares[:, 64:65] / (row.size * devices) + epsilon)
    ).astype(BF16)


def body(
    teacher_rows, teacher_gain, teacher_head, student_rows, student_gain, student_head, lengths
):
    fs = student_head.shape[1]
    vocab = teacher_head.shape[0]
    z = lax.axis_index("z")
    c = lax.axis_index("core")

    block = teacher_rows.T
    wide = block.shape[0]
    values = block.astype(F32)
    scaled = (values * teacher_gain.astype(F32)[:, None]).astype(BF16)
    squares = jnp.stack(split3(jnp.sum(values * values, axis=0)), axis=0)
    sent = jnp.concatenate([scaled, jnp.pad(squares, ((0, HEAD_ROWS - 3), (0, 0)))], axis=0)
    rows = lax.all_gather(sent, ("core", "y"), axis=0, tiled=False)

    heads = jnp.concatenate([student_head.T, teacher_head.T], axis=0)
    own = lax.all_gather(heads, "x", axis=0, tiled=False)
    blocks, offsets = [own], [0]
    mine, theirs = own, swapped(own)
    for step in range(1, NZ // 2):
        mine, theirs = along(mine), along(theirs)
        blocks += [mine, swapped(theirs)]
        offsets += [-step, step]
    blocks.append(along(mine))
    offsets.append(-NZ // 2)

    normed = normalize(student_rows, student_gain).T
    where = jnp.stack([z, 1 - 2 * c])
    missing = offsets[-2:]
    student_logits, teacher_logits, scale, weights = most(
        where, rows, normed, blocks[:-2], offsets[:-2], missing, wide, fs
    )
    student_logits, teacher_logits, lse, weights = last(
        where,
        rows,
        normed,
        blocks[-2:],
        student_logits,
        teacher_logits,
        scale,
        weights,
        missing,
        fs,
    )
    student_w = weights.reshape(NX * NZ * fs, vocab)

    which = jnp.stack([c, lengths[0]])
    lse, which, normed = lax.optimization_barrier((lse, which, normed))
    lse = lax.all_to_all(lse, ("core", "y"), 0, 0, tiled=True)
    other, mine, head_part = gradient(
        which, student_logits, teacher_logits, lse, student_w, normed
    )

    mine = (mine.astype(F32) + swapped(other).astype(F32)).astype(BF16)
    row_grad = lax.psum_scatter(mine, "y", scatter_dimension=0, tiled=True)

    head_part = lax.all_to_all(head_part.reshape(NX, NZ * fs, vocab), "x", 0, 0, tiled=True)
    head_part = jnp.sum(head_part.astype(F32), axis=0).astype(BF16)
    head_part = lax.all_to_all(head_part.reshape(NZ, fs, vocab), "z", 0, 0, tiled=True)

    devices = NX * NZ * NC * NY
    head_grad, squares = pl.pallas_call(
        squares_kernel,
        out_shape=(
            jax.ShapeDtypeStruct((fs, vocab), F32),
            jax.ShapeDtypeStruct((devices, 128), F32),
        ),
    )(head_part, row_grad)
    squares = lax.all_to_all(squares, ("x", "z", "core", "y"), 0, 0, tiled=True)
    head_update, row_update = pl.pallas_call(
        lambda *refs: updates_kernel(devices, *refs),
        out_shape=(
            jax.ShapeDtypeStruct((fs, vocab), BF16),
            jax.ShapeDtypeStruct(row_grad.shape, BF16),
        ),
    )(squares, head_grad, row_grad)
    return (head_update.T, row_update)


def solution(mesh):
    mesh = Mesh(mesh.devices.reshape(NX, NZ, NC, NY), ("x", "z", "core", "y"))
    dp, mp = ("x", "z"), ("core", "y")
    placed = (P(dp, mp), P(mp), P(mp, dp), P(dp, None), P(), P(mp, dp), P(dp))
    return jax.shard_map(
        body,
        mesh=mesh,
        in_specs=placed,
        out_specs=(P(mp, dp), P(dp + mp, None)),
        check_vma=False,
    )
```

```python
import jax
import jax.numpy as jnp
from jax import lax
from jax.experimental import pallas as pl
from jax.experimental.pallas import tpu as pltpu
from jax.sharding import Mesh, PartitionSpec as P

F32 = jnp.float32
BF16 = jnp.bfloat16
DT = 5120
NX, NZ, NC, NY = 4, 8, 2, 8
epsilon = 1e-06
HEAD_ROWS = 16
LSE_ROWS = 8
GRANT = 60 << 20
HBM = pl.BlockSpec(memory_space=pltpu.HBM)
VMEM = pl.BlockSpec(memory_space=pltpu.VMEM)
SMEM = pl.BlockSpec(memory_space=pltpu.SMEM)


def split3(values):
    high = values.astype(BF16)
    rest = values - high.astype(F32)
    middle = rest.astype(BF16)
    low = (rest - middle.astype(F32)).astype(BF16)
    return high, middle, low


def normalize(rows, gain):
    values = rows.astype(F32)
    mean_square = jnp.mean(values * values, axis=-1, keepdims=True)
    return (values * lax.rsqrt(mean_square + epsilon) * gain.astype(F32)).astype(BF16)


def along(values):
    pairs = [(i * NC + c, (i + 1 - 2 * c) % NZ * NC + c) for i in range(NZ) for c in range(NC)]
    return lax.ppermute(values, ("z", "core"), pairs)


def swapped(values):
    return lax.ppermute(values, "core", [(0, 1), (1, 0)])


def against(left, right, dims):
    return lax.dot_general(left, right, (dims, ((), ())), preferred_element_type=F32)


def log_sum_exp(values):
    top = jnp.max(values, axis=0, keepdims=True)
    return top + jnp.log(jnp.sum(jnp.exp(values - top), axis=0, keepdims=True))


def place_of(where_ref, offset):
    return lax.rem(where_ref[0] + where_ref[1] * offset + NZ, NZ)


def begin(copies):
    for copy in copies:
        copy.start()
    return copies


def finish(copies):
    for copy in copies:
        copy.wait()


def block_copies(where_ref, offsets, fs, rows_ref, normed_ref, blocks, held, sems):
    rows, normed, student_w, teacher_w = held
    ft = teacher_w.shape[2]
    per_block = rows_ref.shape[0] // NX
    fold = NZ // per_block
    student, teacher = [], []
    for i, (block, offset) in enumerate(zip(blocks, offsets)):
        at = place_of(where_ref, offset)
        inner = pl.multiple_of(lax.rem(at, fold) * ft, 16)
        copy_sems = sems.at[i]
        student.append(
            pltpu.make_async_copy(block.at[:, pl.ds(0, fs)], student_w.at[:, i], copy_sems.at[0])
        )
        teacher.append(
            pltpu.make_async_copy(block.at[:, pl.ds(fs, ft)], teacher_w.at[:, i], copy_sems.at[1])
        )
        for k in range(NX):
            source = pl.multiple_of(k * NZ * fs + at * fs, 16)
            student.append(
                pltpu.make_async_copy(
                    normed_ref.at[pl.ds(source, fs)], normed.at[k, i], copy_sems.at[2 + k]
                )
            )
            teacher.append(
                pltpu.make_async_copy(
                    rows_ref.at[k * per_block + lax.div(at, fold), pl.ds(inner, ft)],
                    rows.at[k, i],
                    copy_sems.at[2 + NX + k],
                )
            )
    return student, teacher


def weights_copies(where_ref, offsets, student_w, weights_ref, sems):
    return [
        pltpu.make_async_copy(
            student_w.at[:, i], weights_ref.at[:, place_of(where_ref, offset)], sems.at[i]
        )
        for i, offset in enumerate(offsets)
    ]


def product(weights, rows):
    features = weights.shape[1] * weights.shape[2]
    total = None
    for k in range(NX):
        part = against(
            weights[k].reshape(features, weights.shape[3]),
            rows[k].reshape(features, rows.shape[3]),
            ((0,), (0,)),
        )
        total = part if total is None else total + part
    return total


def held_blocks(count, fs, ft, vocab, tokens):
    return [
        pltpu.VMEM((NX, count, ft, tokens), BF16),
        pltpu.VMEM((NX, count, fs, tokens), BF16),
        pltpu.VMEM((NX, count, fs, vocab), BF16),
        pltpu.VMEM((NX, count, ft, vocab), BF16),
        pltpu.VMEM((vocab, tokens), F32),
        pltpu.VMEM((vocab, tokens), F32),
        pltpu.SemaphoreType.DMA((count, 2 + 2 * NX)),
        pltpu.SemaphoreType.DMA((count,)),
        pltpu.SemaphoreType.DMA((4,)),
    ]


def most_kernel(offsets, wide, fs, where_ref, rows_ref, normed_ref, *refs):
    count = len(offsets)
    blocks, refs = refs[:count], refs[count:]
    student_ref, teacher_ref, scale_ref, weights_ref, squares = refs[:5]
    *held, student, teacher, sems, weights_sems, out_sems = refs[5:]
    first, second = block_copies(
        where_ref, offsets, fs, rows_ref, normed_ref, blocks, held, sems
    )
    square_copy = pltpu.make_async_copy(
        rows_ref.at[:, pl.ds(wide, HEAD_ROWS)], squares, out_sems.at[0]
    )
    begin(first + second + [square_copy])
    finish(first)
    out_copies = begin(weights_copies(where_ref, offsets, held[2], weights_ref, weights_sems))
    student[...] = product(held[2], held[1])
    out_copies.append(pltpu.make_async_copy(student, student_ref, out_sems.at[1]))
    out_copies[-1].start()
    finish(second)
    teacher[...] = product(held[3], held[0])
    out_copies.append(pltpu.make_async_copy(teacher, teacher_ref, out_sems.at[2]))
    out_copies[-1].start()
    square_copy.wait()
    square = jnp.sum(jnp.sum(squares[...].astype(F32), axis=0), axis=0, keepdims=True)
    scale_ref[...] = lax.rsqrt(square / DT + epsilon)
    finish(out_copies)


def most(where, rows, normed, blocks, offsets, wide, fs):
    vocab = blocks[0].shape[2]
    ft = blocks[0].shape[1] - fs
    parts, _, tokens = rows.shape

    def kernel(*refs):
        most_kernel(offsets, wide, fs, *refs)

    return pl.pallas_call(
        kernel,
        out_shape=(
            jax.ShapeDtypeStruct((vocab, tokens), F32),
            jax.ShapeDtypeStruct((vocab, tokens), F32),
            jax.ShapeDtypeStruct((1, tokens), F32),
            jax.ShapeDtypeStruct((NX, NZ, fs, vocab), BF16),
        ),
        in_specs=[SMEM, HBM, HBM] + [HBM] * len(blocks),
        out_specs=(HBM, HBM, VMEM, HBM),
        scratch_shapes=[pltpu.VMEM((parts, HEAD_ROWS, tokens), BF16)]
        + held_blocks(len(blocks), fs, ft, vocab, tokens),
        compiler_params=pltpu.CompilerParams(vmem_limit_bytes=GRANT),
        cost_estimate=pl.CostEstimate(
            flops=2 * vocab * tokens * NX * (ft + fs) * len(blocks),
            bytes_accessed=12 << 20,
            transcendentals=0,
        ),
    )(where, rows, normed, *blocks)


def last_kernel(offsets, fs, where_ref, rows_ref, normed_ref, student_part, teacher_part, *refs):
    count = len(offsets)
    scale_ref, _, *blocks = refs[: 2 + count]
    student_ref, teacher_ref, lse_ref, weights_ref = refs[2 + count : 6 + count]
    *held, student, teacher, sems, weights_sems, out_sems = refs[6 + count :]
    first, second = block_copies(
        where_ref, offsets, fs, rows_ref, normed_ref, blocks, held, sems
    )
    first.append(pltpu.make_async_copy(student_part, student, out_sems.at[0]))
    second.append(pltpu.make_async_copy(teacher_part, teacher, out_sems.at[1]))
    begin(first + second)
    finish(first)
    out_copies = begin(weights_copies(where_ref, offsets, held[2], weights_ref, weights_sems))
    total = student[...] + product(held[2], held[1])
    student[...] = total
    out_copies.append(pltpu.make_async_copy(student, student_ref, out_sems.at[2]))
    out_copies[-1].start()
    student_lse = log_sum_exp(total)
    finish(second)
    total = scale_ref[...] * (teacher[...] + product(held[3], held[0]))
    teacher[...] = total
    out_copies.append(pltpu.make_async_copy(teacher, teacher_ref, out_sems.at[3]))
    out_copies[-1].start()
    both = jnp.concatenate([log_sum_exp(total), student_lse], axis=0)
    both = jnp.concatenate([both] * (lse_ref.shape[1] // 2), axis=0)
    lse_ref[...] = jnp.broadcast_to(both[None], lse_ref.shape)
    finish(out_copies)


def last(where, rows, normed, blocks, student, teacher, scale, weights, offsets, fs):
    vocab, tokens = student.shape
    ft = blocks[0].shape[1] - fs

    def kernel(*refs):
        last_kernel(offsets, fs, *refs)

    return pl.pallas_call(
        kernel,
        out_shape=(
            jax.ShapeDtypeStruct((vocab, tokens), F32),
            jax.ShapeDtypeStruct((vocab, tokens), F32),
            jax.ShapeDtypeStruct((NC * NY, LSE_ROWS, tokens), F32),
            jax.ShapeDtypeStruct(weights.shape, BF16),
        ),
        in_specs=[SMEM, HBM, HBM, HBM, HBM, VMEM] + [HBM] * (1 + len(blocks)),
        out_specs=(HBM, HBM, VMEM, HBM),
        input_output_aliases={6: 3},
        scratch_shapes=held_blocks(len(blocks), fs, ft, vocab, tokens),
        compiler_params=pltpu.CompilerParams(vmem_limit_bytes=GRANT),
        cost_estimate=pl.CostEstimate(
            flops=2 * vocab * tokens * NX * (ft + fs) * len(blocks),
            bytes_accessed=8 << 20,
            transcendentals=2 * vocab * tokens,
        ),
    )(where, rows, normed, student, teacher, scale, weights, *blocks)


def grad_kernel(which_ref, student_hbm, teacher_hbm, lse_ref, weights_hbm, *refs):
    other_hbm, mine_hbm, grad_hbm = refs[:3]
    student, teacher, weights, grad_t, turned, other, mine, sems, out_sems = refs[3:]
    copies = begin(
        [
            pltpu.make_async_copy(source, held, sems.at[k])
            for k, (source, held) in enumerate(
                [
                    (student_hbm, student),
                    (teacher_hbm, teacher),
                    (weights_hbm, weights),
                ]
            )
        ]
    )
    tokens = student.shape[1]
    lses = lse_ref[:, 0:2]
    top = jnp.max(lses, axis=0)
    lse = top + jnp.log(jnp.sum(jnp.exp(lses - top[None]), axis=0))
    position = lax.broadcasted_iota(jnp.int32, (1, tokens), 1)
    live = (position < which_ref[1]).astype(F32)
    finish(copies[:2])
    grad = live * (jnp.exp(student[...] - lse[1:2]) - jnp.exp(teacher[...] - lse[0:1]))
    grad_t[...] = grad.astype(BF16)
    turned[...] = grad_t[...].T
    out_copies = begin([pltpu.make_async_copy(grad_t, grad_hbm, out_sems.at[2])])
    half = tokens // NC
    core = which_ref[0]
    parts = [
        (other, other_hbm, turned[pl.ds(pl.multiple_of((1 - core) * half, half), half), :]),
        (mine, mine_hbm, turned[pl.ds(pl.multiple_of(core * half, half), half), :]),
    ]
    width = weights.shape[0] // NX
    slices = [pl.ds(k * width, width) for k in range(NX)]
    copies[2].wait()
    for i, (out, hbm, block) in enumerate(parts):
        for columns in slices:
            out[:, columns] = against(block, weights[columns, :], ((1,), (1,))).astype(BF16)
        out_copies.append(pltpu.make_async_copy(out, hbm, out_sems.at[i]))
        out_copies[-1].start()
    finish(out_copies)


def gradient(which, student, teacher, lse, weights):
    vocab, tokens = student.shape
    features = weights.shape[0]
    half = tokens // NC
    return pl.pallas_call(
        grad_kernel,
        out_shape=(
            jax.ShapeDtypeStruct((half, features), BF16),
            jax.ShapeDtypeStruct((half, features), BF16),
            jax.ShapeDtypeStruct((vocab, tokens), BF16),
        ),
        in_specs=[SMEM, HBM, HBM, VMEM, HBM],
        out_specs=(HBM, HBM, HBM),
        scratch_shapes=[
            pltpu.VMEM((vocab, tokens), F32),
            pltpu.VMEM((vocab, tokens), F32),
            pltpu.VMEM((features, vocab), BF16),
            pltpu.VMEM((vocab, tokens), BF16),
            pltpu.VMEM((tokens, vocab), BF16),
            pltpu.VMEM((half, features), BF16),
            pltpu.VMEM((half, features), BF16),
            pltpu.SemaphoreType.DMA((3,)),
            pltpu.SemaphoreType.DMA((3,)),
        ],
        compiler_params=pltpu.CompilerParams(vmem_limit_bytes=GRANT),
        cost_estimate=pl.CostEstimate(
            flops=2 * vocab * tokens * features,
            bytes_accessed=10 << 20,
            transcendentals=2 * vocab * tokens,
        ),
    )(which, student, teacher, lse, weights)


def head_kernel(normed_hbm, grad_hbm, out_hbm, normed, grad, out, sems, out_sems):
    width = normed.shape[0] // NX
    slices = [pl.ds(k * width, width) for k in range(NX)]
    copies = [pltpu.make_async_copy(grad_hbm, grad, sems.at[NX])]
    copies += [
        pltpu.make_async_copy(normed_hbm.at[rows], normed.at[rows], sems.at[k])
        for k, rows in enumerate(slices)
    ]
    begin(copies)
    copies[0].wait()
    out_copies = []
    for k, rows in enumerate(slices):
        copies[1 + k].wait()
        out[rows, :] = against(normed[rows, :], grad[...], ((1,), (1,))).astype(BF16)
        out_copies.append(pltpu.make_async_copy(out.at[rows], out_hbm.at[rows], out_sems.at[k]))
        out_copies[-1].start()
    finish(out_copies)


def head_product(normed, grad):
    features, vocab = normed.shape[0], grad.shape[0]
    return pl.pallas_call(
        head_kernel,
        out_shape=jax.ShapeDtypeStruct((features, vocab), BF16),
        in_specs=[HBM, HBM],
        out_specs=HBM,
        scratch_shapes=[
            pltpu.VMEM(normed.shape, BF16),
            pltpu.VMEM(grad.shape, BF16),
            pltpu.VMEM((features, vocab), BF16),
            pltpu.SemaphoreType.DMA((1 + NX,)),
            pltpu.SemaphoreType.DMA((NX,)),
        ],
        compiler_params=pltpu.CompilerParams(vmem_limit_bytes=GRANT),
        cost_estimate=pl.CostEstimate(
            flops=2 * vocab * normed.size, bytes_accessed=5 << 20, transcendentals=0
        ),
    )(normed, grad)


def squares_kernel(parts_ref, row_ref, head_ref, out_ref):
    head = jnp.sum(parts_ref[...].astype(F32), axis=0)
    head_ref[...] = head
    row = row_ref[...].astype(F32)
    lane = lax.broadcasted_iota(jnp.int32, out_ref.shape, 1)
    out_ref[...] = jnp.where(lane < 64, jnp.sum(head * head), jnp.sum(row * row))


def updates_kernel(devices, squares_ref, head_ref, row_ref, head_out, row_out):
    squares = jnp.sum(squares_ref[...], axis=0, keepdims=True)
    head = head_ref[...]
    row = row_ref[...].astype(F32)
    head_out[...] = (
        head * lax.rsqrt(squares[:, :1] / (head.size * devices) + epsilon)
    ).astype(BF16)
    row_out[...] = (
        row * lax.rsqrt(squares[:, 64:65] / (row.size * devices) + epsilon)
    ).astype(BF16)


def body(
    teacher_rows, teacher_gain, teacher_head, student_rows, student_gain, student_head, lengths
):
    fs = student_head.shape[1]
    vocab = teacher_head.shape[0]
    z = lax.axis_index("z")
    c = lax.axis_index("core")

    block = teacher_rows.T
    wide = block.shape[0]
    values = block.astype(F32)
    scaled = (values * teacher_gain.astype(F32)[:, None]).astype(BF16)
    squares = jnp.stack(split3(jnp.sum(values * values, axis=0)), axis=0)
    sent = jnp.concatenate([scaled, jnp.pad(squares, ((0, HEAD_ROWS - 3), (0, 0)))], axis=0)
    rows = lax.all_gather(sent, ("core", "y"), axis=0, tiled=False)

    normed = normalize(student_rows, student_gain).T
    heads = jnp.concatenate([student_head.T, teacher_head.T], axis=0)
    own = lax.all_gather(heads, "x", axis=0, tiled=False)
    blocks, offsets = [own], [0]
    mine, theirs = own, swapped(own)
    for step in range(1, NZ // 2):
        mine, theirs = along(mine), along(theirs)
        if step == 1:
            theirs, normed = lax.optimization_barrier((theirs, normed))
        if step < NZ // 2 - 1:
            blocks += [mine, swapped(theirs)]
            offsets += [-step, step]

    early = len(blocks)
    where = jnp.stack([z, 1 - 2 * c])
    student_logits, teacher_logits, scale, weights = most(
        where, rows, normed, blocks[:early], offsets[:early], wide, fs
    )
    mine, theirs, student_logits, teacher_logits, scale, weights = lax.optimization_barrier(
        (mine, theirs, student_logits, teacher_logits, scale, weights)
    )
    blocks += [mine, swapped(theirs), along(mine)]
    offsets += [1 - NZ // 2, NZ // 2 - 1, -NZ // 2]
    student_logits, teacher_logits, lse, weights = last(
        where,
        rows,
        normed,
        blocks[early:],
        student_logits,
        teacher_logits,
        scale,
        weights,
        offsets[early:],
        fs,
    )
    student_w = weights.reshape(NX * NZ * fs, vocab)

    which = jnp.stack([c, lengths[0]])
    lse, which, normed = lax.optimization_barrier((lse, which, normed))
    lse = lax.all_to_all(lse, ("core", "y"), 0, 0, tiled=True)
    other, mine, logit_grad = gradient(which, student_logits, teacher_logits, lse, student_w)
    other = swapped(other)
    head_part = head_product(normed, logit_grad)

    mine = (mine.astype(F32) + other.astype(F32)).astype(BF16)
    row_grad = lax.psum_scatter(mine, "y", scatter_dimension=0, tiled=True)

    head_part = lax.all_to_all(head_part.reshape(NX, NZ * fs, vocab), "x", 0, 0, tiled=True)
    head_part = jnp.sum(head_part.astype(F32), axis=0).astype(BF16)
    head_part = lax.all_to_all(head_part.reshape(NZ, fs, vocab), "z", 0, 0, tiled=True)

    devices = NX * NZ * NC * NY
    head_grad, squares = pl.pallas_call(
        squares_kernel,
        out_shape=(
            jax.ShapeDtypeStruct((fs, vocab), F32),
            jax.ShapeDtypeStruct((devices, 128), F32),
        ),
    )(head_part, row_grad)
    squares = lax.all_to_all(squares, ("x", "z", "core", "y"), 0, 0, tiled=True)
    head_update, row_update = pl.pallas_call(
        lambda *refs: updates_kernel(devices, *refs),
        out_shape=(
            jax.ShapeDtypeStruct((fs, vocab), BF16),
            jax.ShapeDtypeStruct(row_grad.shape, BF16),
        ),
    )(squares, head_grad, row_grad)
    return (head_update.T, row_update)


def solution(mesh):
    mesh = Mesh(mesh.devices.reshape(NX, NZ, NC, NY), ("x", "z", "core", "y"))
    dp, mp = ("x", "z"), ("core", "y")
    placed = (P(dp, mp), P(mp), P(mp, dp), P(dp, None), P(), P(mp, dp), P(dp))
    return jax.shard_map(
        body,
        mesh=mesh,
        in_specs=placed,
        out_specs=(P(mp, dp), P(dp + mp, None)),
        check_vma=False,
    )
```

```python
import jax
import jax.numpy as jnp
from jax import lax
from jax.experimental import pallas as pl
from jax.experimental.pallas import tpu as pltpu
from jax.sharding import Mesh, PartitionSpec as P

F32 = jnp.float32
BF16 = jnp.bfloat16
DT = 5120
NX, NZ, NC, NY = 4, 8, 2, 8
epsilon = 1e-06
HEAD_ROWS = 16
LSE_ROWS = 8
GRANT = 60 << 20
HBM = pl.BlockSpec(memory_space=pltpu.HBM)
VMEM = pl.BlockSpec(memory_space=pltpu.VMEM)
SMEM = pl.BlockSpec(memory_space=pltpu.SMEM)


def split3(values):
    high = values.astype(BF16)
    rest = values - high.astype(F32)
    middle = rest.astype(BF16)
    low = (rest - middle.astype(F32)).astype(BF16)
    return high, middle, low


def normalize(rows, gain):
    values = rows.astype(F32)
    mean_square = jnp.mean(values * values, axis=-1, keepdims=True)
    return (values * lax.rsqrt(mean_square + epsilon) * gain.astype(F32)).astype(BF16)


def along(values):
    pairs = [(i * NC + c, (i + 1 - 2 * c) % NZ * NC + c) for i in range(NZ) for c in range(NC)]
    return lax.ppermute(values, ("z", "core"), pairs)


def swapped(values):
    return lax.ppermute(values, "core", [(0, 1), (1, 0)])


def against(left, right, dims):
    return lax.dot_general(left, right, (dims, ((), ())), preferred_element_type=F32)


def log_sum_exp(values):
    top = jnp.max(values, axis=0, keepdims=True)
    return top + jnp.log(jnp.sum(jnp.exp(values - top), axis=0, keepdims=True))


def place_of(where_ref, offset):
    return lax.rem(where_ref[0] + where_ref[1] * offset + NZ, NZ)


def begin(copies):
    for copy in copies:
        copy.start()
    return copies


def finish(copies):
    for copy in copies:
        copy.wait()


def block_copies(where_ref, offsets, fs, rows_ref, normed_ref, blocks, held, sems):
    rows, normed, student_w, teacher_w = held
    ft = teacher_w.shape[2]
    per_block = rows_ref.shape[0] // NX
    fold = NZ // per_block
    student, teacher = [], []
    for i, (block, offset) in enumerate(zip(blocks, offsets)):
        at = place_of(where_ref, offset)
        inner = pl.multiple_of(lax.rem(at, fold) * ft, 16)
        copy_sems = sems.at[i]
        student.append(
            pltpu.make_async_copy(block.at[:, pl.ds(0, fs)], student_w.at[:, i], copy_sems.at[0])
        )
        teacher.append(
            pltpu.make_async_copy(block.at[:, pl.ds(fs, ft)], teacher_w.at[:, i], copy_sems.at[1])
        )
        for k in range(NX):
            source = pl.multiple_of(k * NZ * fs + at * fs, 16)
            student.append(
                pltpu.make_async_copy(
                    normed_ref.at[pl.ds(source, fs)], normed.at[k, i], copy_sems.at[2 + k]
                )
            )
            teacher.append(
                pltpu.make_async_copy(
                    rows_ref.at[k * per_block + lax.div(at, fold), pl.ds(inner, ft)],
                    rows.at[k, i],
                    copy_sems.at[2 + NX + k],
                )
            )
    return student, teacher


def weights_copies(where_ref, offsets, student_w, weights_ref, sems):
    return [
        pltpu.make_async_copy(
            student_w.at[:, i], weights_ref.at[:, place_of(where_ref, offset)], sems.at[i]
        )
        for i, offset in enumerate(offsets)
    ]


def product(weights, rows):
    features = weights.shape[1] * weights.shape[2]
    total = None
    for k in range(NX):
        part = against(
            weights[k].reshape(features, weights.shape[3]),
            rows[k].reshape(features, rows.shape[3]),
            ((0,), (0,)),
        )
        total = part if total is None else total + part
    return total


def held_blocks(count, fs, ft, vocab, tokens):
    return [
        pltpu.VMEM((NX, count, ft, tokens), BF16),
        pltpu.VMEM((NX, count, fs, tokens), BF16),
        pltpu.VMEM((NX, count, fs, vocab), BF16),
        pltpu.VMEM((NX, count, ft, vocab), BF16),
        pltpu.VMEM((vocab, tokens), F32),
        pltpu.VMEM((vocab, tokens), F32),
        pltpu.SemaphoreType.DMA((count, 2 + 2 * NX)),
        pltpu.SemaphoreType.DMA((count,)),
        pltpu.SemaphoreType.DMA((4,)),
    ]


def most_kernel(offsets, wide, fs, where_ref, rows_ref, normed_ref, *refs):
    count = len(offsets)
    blocks, refs = refs[:count], refs[count:]
    student_ref, teacher_ref, scale_ref, weights_ref, squares = refs[:5]
    *held, student, teacher, sems, weights_sems, out_sems = refs[5:]
    first, second = block_copies(
        where_ref, offsets, fs, rows_ref, normed_ref, blocks, held, sems
    )
    square_copy = pltpu.make_async_copy(
        rows_ref.at[:, pl.ds(wide, HEAD_ROWS)], squares, out_sems.at[0]
    )
    begin(first + second + [square_copy])
    finish(first)
    out_copies = begin(weights_copies(where_ref, offsets, held[2], weights_ref, weights_sems))
    student[...] = product(held[2], held[1])
    out_copies.append(pltpu.make_async_copy(student, student_ref, out_sems.at[1]))
    out_copies[-1].start()
    finish(second)
    teacher[...] = product(held[3], held[0])
    out_copies.append(pltpu.make_async_copy(teacher, teacher_ref, out_sems.at[2]))
    out_copies[-1].start()
    square_copy.wait()
    square = jnp.sum(jnp.sum(squares[...].astype(F32), axis=0), axis=0, keepdims=True)
    scale_ref[...] = lax.rsqrt(square / DT + epsilon)
    finish(out_copies)


def most(where, rows, normed, blocks, offsets, wide, fs):
    vocab = blocks[0].shape[2]
    ft = blocks[0].shape[1] - fs
    parts, _, tokens = rows.shape

    def kernel(*refs):
        most_kernel(offsets, wide, fs, *refs)

    return pl.pallas_call(
        kernel,
        out_shape=(
            jax.ShapeDtypeStruct((vocab, tokens), F32),
            jax.ShapeDtypeStruct((vocab, tokens), F32),
            jax.ShapeDtypeStruct((1, tokens), F32),
            jax.ShapeDtypeStruct((NX, NZ, fs, vocab), BF16),
        ),
        in_specs=[SMEM, HBM, HBM] + [HBM] * len(blocks),
        out_specs=(HBM, HBM, VMEM, HBM),
        scratch_shapes=[pltpu.VMEM((parts, HEAD_ROWS, tokens), BF16)]
        + held_blocks(len(blocks), fs, ft, vocab, tokens),
        compiler_params=pltpu.CompilerParams(vmem_limit_bytes=GRANT),
        cost_estimate=pl.CostEstimate(
            flops=2 * vocab * tokens * NX * (ft + fs) * len(blocks),
            bytes_accessed=12 << 20,
            transcendentals=0,
        ),
    )(where, rows, normed, *blocks)


def last_kernel(offsets, fs, where_ref, rows_ref, normed_ref, student_part, teacher_part, *refs):
    count = len(offsets)
    scale_ref, _, *blocks = refs[: 2 + count]
    student_ref, teacher_ref, lse_ref, weights_ref = refs[2 + count : 6 + count]
    *held, student, teacher, sems, weights_sems, out_sems = refs[6 + count :]
    first, second = block_copies(
        where_ref, offsets, fs, rows_ref, normed_ref, blocks, held, sems
    )
    first.append(pltpu.make_async_copy(student_part, student, out_sems.at[0]))
    second.append(pltpu.make_async_copy(teacher_part, teacher, out_sems.at[1]))
    begin(first + second)
    finish(first)
    out_copies = begin(weights_copies(where_ref, offsets, held[2], weights_ref, weights_sems))
    total = student[...] + product(held[2], held[1])
    student[...] = total
    out_copies.append(pltpu.make_async_copy(student, student_ref, out_sems.at[2]))
    out_copies[-1].start()
    student_lse = log_sum_exp(total)
    finish(second)
    total = scale_ref[...] * (teacher[...] + product(held[3], held[0]))
    teacher[...] = total
    out_copies.append(pltpu.make_async_copy(teacher, teacher_ref, out_sems.at[3]))
    out_copies[-1].start()
    both = jnp.concatenate([log_sum_exp(total), student_lse], axis=0)
    both = jnp.concatenate([both] * (lse_ref.shape[1] // 2), axis=0)
    lse_ref[...] = jnp.broadcast_to(both[None], lse_ref.shape)
    finish(out_copies)


def last(where, rows, normed, blocks, student, teacher, scale, weights, offsets, fs):
    vocab, tokens = student.shape
    ft = blocks[0].shape[1] - fs

    def kernel(*refs):
        last_kernel(offsets, fs, *refs)

    return pl.pallas_call(
        kernel,
        out_shape=(
            jax.ShapeDtypeStruct((vocab, tokens), F32),
            jax.ShapeDtypeStruct((vocab, tokens), F32),
            jax.ShapeDtypeStruct((NC * NY, LSE_ROWS, tokens), F32),
            jax.ShapeDtypeStruct(weights.shape, BF16),
        ),
        in_specs=[SMEM, HBM, HBM, HBM, HBM, VMEM] + [HBM] * (1 + len(blocks)),
        out_specs=(HBM, HBM, VMEM, HBM),
        input_output_aliases={6: 3},
        scratch_shapes=held_blocks(len(blocks), fs, ft, vocab, tokens),
        compiler_params=pltpu.CompilerParams(vmem_limit_bytes=GRANT),
        cost_estimate=pl.CostEstimate(
            flops=2 * vocab * tokens * NX * (ft + fs) * len(blocks),
            bytes_accessed=8 << 20,
            transcendentals=2 * vocab * tokens,
        ),
    )(where, rows, normed, student, teacher, scale, weights, *blocks)


def grad_kernel(which_ref, student_hbm, teacher_hbm, lse_ref, weights_hbm, normed_hbm, *refs):
    other_hbm, mine_hbm, head_hbm = refs[:3]
    student, teacher, weights, normed, grad_t, turned, other, mine, head, sems, out_sems = refs[3:]
    copies = begin(
        [
            pltpu.make_async_copy(source, held, sems.at[k])
            for k, (source, held) in enumerate(
                [
                    (student_hbm, student),
                    (teacher_hbm, teacher),
                    (weights_hbm, weights),
                    (normed_hbm, normed),
                ]
            )
        ]
    )
    tokens = student.shape[1]
    lses = lse_ref[:, 0:2]
    top = jnp.max(lses, axis=0)
    lse = top + jnp.log(jnp.sum(jnp.exp(lses - top[None]), axis=0))
    position = lax.broadcasted_iota(jnp.int32, (1, tokens), 1)
    live = (position < which_ref[1]).astype(F32)
    finish(copies[:2])
    grad = live * (jnp.exp(student[...] - lse[1:2]) - jnp.exp(teacher[...] - lse[0:1]))
    grad_t[...] = grad.astype(BF16)
    turned[...] = grad_t[...].T
    half = tokens // NC
    core = which_ref[0]
    parts = [
        (other, other_hbm, turned[pl.ds(pl.multiple_of((1 - core) * half, half), half), :]),
        (mine, mine_hbm, turned[pl.ds(pl.multiple_of(core * half, half), half), :]),
    ]
    width = weights.shape[0] // NX
    slices = [pl.ds(k * width, width) for k in range(NX)]
    copies[2].wait()
    out_copies = []
    for i, (out, hbm, block) in enumerate(parts):
        for columns in slices:
            out[:, columns] = against(block, weights[columns, :], ((1,), (1,))).astype(BF16)
        out_copies.append(pltpu.make_async_copy(out, hbm, out_sems.at[i]))
        out_copies[-1].start()
    copies[3].wait()
    for k, rows in enumerate(slices):
        head[rows, :] = against(normed[rows, :], grad_t[...], ((1,), (1,))).astype(BF16)
        out_copies.append(pltpu.make_async_copy(head.at[rows], head_hbm.at[rows], out_sems.at[2 + k]))
        out_copies[-1].start()
    finish(out_copies)


def gradient(which, student, teacher, lse, weights, normed):
    vocab, tokens = student.shape
    features = weights.shape[0]
    half = tokens // NC
    return pl.pallas_call(
        grad_kernel,
        out_shape=(
            jax.ShapeDtypeStruct((half, features), BF16),
            jax.ShapeDtypeStruct((half, features), BF16),
            jax.ShapeDtypeStruct((features, vocab), BF16),
        ),
        in_specs=[SMEM, HBM, HBM, VMEM, HBM, HBM],
        out_specs=(HBM, HBM, HBM),
        scratch_shapes=[
            pltpu.VMEM((vocab, tokens), F32),
            pltpu.VMEM((vocab, tokens), F32),
            pltpu.VMEM((features, vocab), BF16),
            pltpu.VMEM((features, tokens), BF16),
            pltpu.VMEM((vocab, tokens), BF16),
            pltpu.VMEM((tokens, vocab), BF16),
            pltpu.VMEM((half, features), BF16),
            pltpu.VMEM((half, features), BF16),
            pltpu.VMEM((features, vocab), BF16),
            pltpu.SemaphoreType.DMA((4,)),
            pltpu.SemaphoreType.DMA((2 + NX,)),
        ],
        compiler_params=pltpu.CompilerParams(vmem_limit_bytes=GRANT),
        cost_estimate=pl.CostEstimate(
            flops=4 * vocab * tokens * features,
            bytes_accessed=10 << 20,
            transcendentals=2 * vocab * tokens,
        ),
    )(which, student, teacher, lse, weights, normed)


def squares_kernel(parts_ref, row_ref, head_ref, out_ref):
    head = jnp.sum(parts_ref[...].astype(F32), axis=0)
    head_ref[...] = head
    row = row_ref[...].astype(F32)
    lane = lax.broadcasted_iota(jnp.int32, out_ref.shape, 1)
    out_ref[...] = jnp.where(lane < 64, jnp.sum(head * head), jnp.sum(row * row))


def updates_kernel(devices, squares_ref, head_ref, row_ref, head_out, row_out):
    squares = jnp.sum(squares_ref[...], axis=0, keepdims=True)
    head = head_ref[...]
    row = row_ref[...].astype(F32)
    head_out[...] = (
        head * lax.rsqrt(squares[:, :1] / (head.size * devices) + epsilon)
    ).astype(BF16)
    row_out[...] = (
        row * lax.rsqrt(squares[:, 64:65] / (row.size * devices) + epsilon)
    ).astype(BF16)


def body(
    teacher_rows, teacher_gain, teacher_head, student_rows, student_gain, student_head, lengths
):
    fs = student_head.shape[1]
    vocab = teacher_head.shape[0]
    z = lax.axis_index("z")
    c = lax.axis_index("core")

    block = teacher_rows.T
    wide = block.shape[0]
    values = block.astype(F32)
    scaled = (values * teacher_gain.astype(F32)[:, None]).astype(BF16)
    squares = jnp.stack(split3(jnp.sum(values * values, axis=0)), axis=0)
    sent = jnp.concatenate([scaled, jnp.pad(squares, ((0, HEAD_ROWS - 3), (0, 0)))], axis=0)
    rows = lax.all_gather(sent, ("core", "y"), axis=0, tiled=False)

    heads = jnp.concatenate([student_head.T, teacher_head.T], axis=0)
    own = lax.all_gather(heads, "x", axis=0, tiled=False)
    blocks, offsets = [own], [0]
    mine, theirs = own, swapped(own)
    for step in range(1, NZ // 2):
        mine, theirs = along(mine), along(theirs)
        if step < NZ // 2 - 1:
            blocks += [mine, swapped(theirs)]
            offsets += [-step, step]

    normed = normalize(student_rows, student_gain).T
    early = len(blocks)
    blocks += [mine, along(mine)]
    offsets += [1 - NZ // 2, -NZ // 2]
    where = jnp.stack([z, 1 - 2 * c])
    student_logits, teacher_logits, scale, weights = most(
        where, rows, normed, blocks[:early], offsets[:early], wide, fs
    )
    theirs, student_logits, teacher_logits, scale, weights = lax.optimization_barrier(
        (theirs, student_logits, teacher_logits, scale, weights)
    )
    blocks.append(swapped(theirs))
    offsets.append(NZ // 2 - 1)
    student_logits, teacher_logits, lse, weights = last(
        where,
        rows,
        normed,
        blocks[early:],
        student_logits,
        teacher_logits,
        scale,
        weights,
        offsets[early:],
        fs,
    )
    student_w = weights.reshape(NX * NZ * fs, vocab)

    which = jnp.stack([c, lengths[0]])
    lse, which, normed = lax.optimization_barrier((lse, which, normed))
    lse = lax.all_to_all(lse, ("core", "y"), 0, 0, tiled=True)
    other, mine, head_part = gradient(
        which, student_logits, teacher_logits, lse, student_w, normed
    )

    other = swapped(other)
    mine = (mine.astype(F32) + other.astype(F32)).astype(BF16)
    row_grad = lax.psum_scatter(mine, "y", scatter_dimension=0, tiled=True)

    head_part = lax.all_to_all(head_part.reshape(NX, NZ * fs, vocab), "x", 0, 0, tiled=True)
    head_part = jnp.sum(head_part.astype(F32), axis=0).astype(BF16)
    head_part = lax.all_to_all(head_part.reshape(NZ, fs, vocab), "z", 0, 0, tiled=True)

    devices = NX * NZ * NC * NY
    head_grad, squares = pl.pallas_call(
        squares_kernel,
        out_shape=(
            jax.ShapeDtypeStruct((fs, vocab), F32),
            jax.ShapeDtypeStruct((devices, 128), F32),
        ),
    )(head_part, row_grad)
    squares = lax.all_to_all(squares, ("x", "z", "core", "y"), 0, 0, tiled=True)
    head_update, row_update = pl.pallas_call(
        lambda *refs: updates_kernel(devices, *refs),
        out_shape=(
            jax.ShapeDtypeStruct((fs, vocab), BF16),
            jax.ShapeDtypeStruct(row_grad.shape, BF16),
        ),
    )(squares, head_grad, row_grad)
    return (head_update.T, row_update)


def solution(mesh):
    mesh = Mesh(mesh.devices.reshape(NX, NZ, NC, NY), ("x", "z", "core", "y"))
    dp, mp = ("x", "z"), ("core", "y")
    placed = (P(dp, mp), P(mp), P(mp, dp), P(dp, None), P(), P(mp, dp), P(dp))
    return jax.shard_map(
        body,
        mesh=mesh,
        in_specs=placed,
        out_specs=(P(mp, dp), P(dp + mp, None)),
        check_vma=False,
    )
```

```python
import jax
import jax.numpy as jnp
from jax import lax
from jax.experimental import pallas as pl
from jax.experimental.pallas import tpu as pltpu
from jax.sharding import Mesh, PartitionSpec as P

F32 = jnp.float32
BF16 = jnp.bfloat16
DT = 5120
NX, NZ, NC, NY = 4, 8, 2, 8
epsilon = 1e-06
HEAD_ROWS = 16
LSE_ROWS = 2
GRANT = 60 << 20
HBM = pl.BlockSpec(memory_space=pltpu.HBM)
VMEM = pl.BlockSpec(memory_space=pltpu.VMEM)
SMEM = pl.BlockSpec(memory_space=pltpu.SMEM)


def split3(values):
    high = values.astype(BF16)
    rest = values - high.astype(F32)
    middle = rest.astype(BF16)
    low = (rest - middle.astype(F32)).astype(BF16)
    return high, middle, low


def scaled_kernel(rows_ref, gain_ref, out_ref):
    values = rows_ref[...].astype(F32)
    wide = values.shape[0]
    gain = jnp.broadcast_to(gain_ref[...].astype(F32), (128, wide)).T[:, :1]
    out_ref[pl.ds(0, wide), :] = (values * gain).astype(BF16)
    terms = split3(jnp.sum(values * values, axis=0, keepdims=True))
    rest = jnp.zeros((HEAD_ROWS - len(terms), values.shape[1]), F32)
    terms = jnp.concatenate([term.astype(F32) for term in terms] + [rest], axis=0)
    out_ref[pl.ds(wide, HEAD_ROWS), :] = terms.astype(BF16)


def normalize(rows, gain):
    values = rows.astype(F32)
    mean_square = jnp.mean(values * values, axis=-1, keepdims=True)
    return (values * lax.rsqrt(mean_square + epsilon) * gain.astype(F32)).astype(BF16)


def along(values):
    pairs = [(i * NC + c, (i + 1 - 2 * c) % NZ * NC + c) for i in range(NZ) for c in range(NC)]
    return lax.ppermute(values, ("z", "core"), pairs)


def swapped(values):
    return lax.ppermute(values, "core", [(0, 1), (1, 0)])


def against(left, right, dims):
    return lax.dot_general(left, right, (dims, ((), ())), preferred_element_type=F32)


def log_sum_exp(values):
    top = jnp.max(values, axis=0, keepdims=True)
    return top + jnp.log(jnp.sum(jnp.exp(values - top), axis=0, keepdims=True))


def place_of(where_ref, offset):
    return lax.rem(where_ref[0] + where_ref[1] * offset + NZ, NZ)


def begin(copies):
    for copy in copies:
        copy.start()
    return copies


def finish(copies):
    for copy in copies:
        copy.wait()


def block_copies(where_ref, offsets, fs, rows_ref, normed_ref, blocks, held, sems):
    rows, normed, student_w, teacher_w = held
    ft = teacher_w.shape[2]
    per_block = rows_ref.shape[0] // NX
    fold = NZ // per_block
    student, teacher = [], []
    for i, (block, offset) in enumerate(zip(blocks, offsets)):
        at = place_of(where_ref, offset)
        inner = pl.multiple_of(lax.rem(at, fold) * ft, 16)
        copy_sems = sems.at[i]
        student.append(
            pltpu.make_async_copy(block.at[:, pl.ds(0, fs)], student_w.at[:, i], copy_sems.at[0])
        )
        teacher.append(
            pltpu.make_async_copy(block.at[:, pl.ds(fs, ft)], teacher_w.at[:, i], copy_sems.at[1])
        )
        for k in range(NX):
            source = pl.multiple_of(k * NZ * fs + at * fs, 16)
            student.append(
                pltpu.make_async_copy(
                    normed_ref.at[pl.ds(source, fs)], normed.at[k, i], copy_sems.at[2 + k]
                )
            )
            teacher.append(
                pltpu.make_async_copy(
                    rows_ref.at[k * per_block + lax.div(at, fold), pl.ds(inner, ft)],
                    rows.at[k, i],
                    copy_sems.at[2 + NX + k],
                )
            )
    return student, teacher


def weights_copies(where_ref, offsets, student_w, weights_ref, sems):
    return [
        pltpu.make_async_copy(
            student_w.at[:, i], weights_ref.at[:, place_of(where_ref, offset)], sems.at[i]
        )
        for i, offset in enumerate(offsets)
    ]


def product(weights, rows):
    features = weights.shape[1] * weights.shape[2]
    total = None
    for k in range(NX):
        part = against(
            weights[k].reshape(features, weights.shape[3]),
            rows[k].reshape(features, rows.shape[3]),
            ((0,), (0,)),
        )
        total = part if total is None else total + part
    return total


def held_blocks(count, fs, ft, vocab, tokens):
    return [
        pltpu.VMEM((NX, count, ft, tokens), BF16),
        pltpu.VMEM((NX, count, fs, tokens), BF16),
        pltpu.VMEM((NX, count, fs, vocab), BF16),
        pltpu.VMEM((NX, count, ft, vocab), BF16),
        pltpu.VMEM((vocab, tokens), F32),
        pltpu.VMEM((vocab, tokens), F32),
        pltpu.SemaphoreType.DMA((count, 2 + 2 * NX)),
        pltpu.SemaphoreType.DMA((count,)),
        pltpu.SemaphoreType.DMA((4,)),
    ]


def most_kernel(offsets, wide, fs, where_ref, rows_ref, normed_ref, *refs):
    count = len(offsets)
    blocks, refs = refs[:count], refs[count:]
    student_ref, teacher_ref, scale_ref, weights_ref, squares = refs[:5]
    *held, student, teacher, sems, weights_sems, out_sems = refs[5:]
    first, second = block_copies(
        where_ref, offsets, fs, rows_ref, normed_ref, blocks, held, sems
    )
    square_copy = pltpu.make_async_copy(
        rows_ref.at[:, pl.ds(wide, HEAD_ROWS)], squares, out_sems.at[0]
    )
    begin(first + second + [square_copy])
    finish(first)
    out_copies = begin(weights_copies(where_ref, offsets, held[2], weights_ref, weights_sems))
    student[...] = product(held[2], held[1])
    out_copies.append(pltpu.make_async_copy(student, student_ref, out_sems.at[1]))
    out_copies[-1].start()
    finish(second)
    teacher[...] = product(held[3], held[0])
    out_copies.append(pltpu.make_async_copy(teacher, teacher_ref, out_sems.at[2]))
    out_copies[-1].start()
    square_copy.wait()
    square = jnp.sum(jnp.sum(squares[...].astype(F32), axis=0), axis=0, keepdims=True)
    scale_ref[...] = lax.rsqrt(square / DT + epsilon)
    finish(out_copies)


def most(where, rows, normed, blocks, offsets, wide, fs):
    vocab = blocks[0].shape[2]
    ft = blocks[0].shape[1] - fs
    parts, _, tokens = rows.shape

    def kernel(*refs):
        most_kernel(offsets, wide, fs, *refs)

    return pl.pallas_call(
        kernel,
        out_shape=(
            jax.ShapeDtypeStruct((vocab, tokens), F32),
            jax.ShapeDtypeStruct((vocab, tokens), F32),
            jax.ShapeDtypeStruct((1, tokens), F32),
            jax.ShapeDtypeStruct((NX, NZ, fs, vocab), BF16),
        ),
        in_specs=[SMEM, HBM, HBM] + [HBM] * len(blocks),
        out_specs=(HBM, HBM, VMEM, HBM),
        scratch_shapes=[pltpu.VMEM((parts, HEAD_ROWS, tokens), BF16)]
        + held_blocks(len(blocks), fs, ft, vocab, tokens),
        compiler_params=pltpu.CompilerParams(vmem_limit_bytes=GRANT),
        cost_estimate=pl.CostEstimate(
            flops=2 * vocab * tokens * NX * (ft + fs) * len(blocks),
            bytes_accessed=12 << 20,
            transcendentals=0,
        ),
    )(where, rows, normed, *blocks)


def last_kernel(offsets, fs, where_ref, rows_ref, normed_ref, student_part, teacher_part, *refs):
    count = len(offsets)
    scale_ref, _, *blocks = refs[: 2 + count]
    student_ref, teacher_ref, lse_ref, weights_ref = refs[2 + count : 6 + count]
    *held, student, teacher, sems, weights_sems, out_sems = refs[6 + count :]
    first, second = block_copies(
        where_ref, offsets, fs, rows_ref, normed_ref, blocks, held, sems
    )
    first.append(pltpu.make_async_copy(student_part, student, out_sems.at[0]))
    second.append(pltpu.make_async_copy(teacher_part, teacher, out_sems.at[1]))
    begin(first + second)
    finish(first)
    out_copies = begin(weights_copies(where_ref, offsets, held[2], weights_ref, weights_sems))
    total = student[...] + product(held[2], held[1])
    student[...] = total
    out_copies.append(pltpu.make_async_copy(student, student_ref, out_sems.at[2]))
    out_copies[-1].start()
    student_lse = log_sum_exp(total)
    finish(second)
    total = scale_ref[...] * (teacher[...] + product(held[3], held[0]))
    teacher[...] = total
    out_copies.append(pltpu.make_async_copy(teacher, teacher_ref, out_sems.at[3]))
    out_copies[-1].start()
    both = jnp.concatenate([log_sum_exp(total), student_lse], axis=0)
    both = jnp.concatenate([both] * (lse_ref.shape[1] // 2), axis=0)
    lse_ref[...] = jnp.broadcast_to(both[None], lse_ref.shape)
    finish(out_copies)


def last(where, rows, normed, blocks, student, teacher, scale, weights, offsets, fs):
    vocab, tokens = student.shape
    ft = blocks[0].shape[1] - fs

    def kernel(*refs):
        last_kernel(offsets, fs, *refs)

    return pl.pallas_call(
        kernel,
        out_shape=(
            jax.ShapeDtypeStruct((vocab, tokens), F32),
            jax.ShapeDtypeStruct((vocab, tokens), F32),
            jax.ShapeDtypeStruct((NC * NY, LSE_ROWS, tokens), F32),
            jax.ShapeDtypeStruct(weights.shape, BF16),
        ),
        in_specs=[SMEM, HBM, HBM, HBM, HBM, VMEM] + [HBM] * (1 + len(blocks)),
        out_specs=(HBM, HBM, VMEM, HBM),
        input_output_aliases={6: 3},
        scratch_shapes=held_blocks(len(blocks), fs, ft, vocab, tokens),
        compiler_params=pltpu.CompilerParams(vmem_limit_bytes=GRANT),
        cost_estimate=pl.CostEstimate(
            flops=2 * vocab * tokens * NX * (ft + fs) * len(blocks),
            bytes_accessed=8 << 20,
            transcendentals=2 * vocab * tokens,
        ),
    )(where, rows, normed, student, teacher, scale, weights, *blocks)


def grad_kernel(which_ref, student_hbm, teacher_hbm, lse_ref, weights_hbm, normed_hbm, *refs):
    other_hbm, mine_hbm, head_hbm = refs[:3]
    student, teacher, weights, normed, grad_t, turned, other, mine, head, sems, out_sems = refs[3:]
    copies = begin(
        [
            pltpu.make_async_copy(source, held, sems.at[k])
            for k, (source, held) in enumerate(
                [
                    (student_hbm, student),
                    (teacher_hbm, teacher),
                    (weights_hbm, weights),
                    (normed_hbm, normed),
                ]
            )
        ]
    )
    tokens = student.shape[1]
    lses = lse_ref[:, 0:2]
    top = jnp.max(lses, axis=0)
    lse = top + jnp.log(jnp.sum(jnp.exp(lses - top[None]), axis=0))
    position = lax.broadcasted_iota(jnp.int32, (1, tokens), 1)
    live = (position < which_ref[1]).astype(F32)
    finish(copies[:2])
    grad = live * (jnp.exp(student[...] - lse[1:2]) - jnp.exp(teacher[...] - lse[0:1]))
    grad_t[...] = grad.astype(BF16)
    turned[...] = grad_t[...].T
    half = tokens // NC
    core = which_ref[0]
    parts = [
        (other, other_hbm, turned[pl.ds(pl.multiple_of((1 - core) * half, half), half), :]),
        (mine, mine_hbm, turned[pl.ds(pl.multiple_of(core * half, half), half), :]),
    ]
    width = weights.shape[0] // NX
    slices = [pl.ds(k * width, width) for k in range(NX)]
    copies[2].wait()
    out_copies = []
    for i, (out, hbm, block) in enumerate(parts):
        for columns in slices:
            out[:, columns] = against(block, weights[columns, :], ((1,), (1,))).astype(BF16)
        out_copies.append(pltpu.make_async_copy(out, hbm, out_sems.at[i]))
        out_copies[-1].start()
    copies[3].wait()
    for k, rows in enumerate(slices):
        head[rows, :] = against(normed[rows, :], grad_t[...], ((1,), (1,))).astype(BF16)
        out_copies.append(pltpu.make_async_copy(head.at[rows], head_hbm.at[rows], out_sems.at[2 + k]))
        out_copies[-1].start()
    finish(out_copies)


def gradient(which, student, teacher, lse, weights, normed):
    vocab, tokens = student.shape
    features = weights.shape[0]
    half = tokens // NC
    return pl.pallas_call(
        grad_kernel,
        out_shape=(
            jax.ShapeDtypeStruct((half, features), BF16),
            jax.ShapeDtypeStruct((half, features), BF16),
            jax.ShapeDtypeStruct((features, vocab), BF16),
        ),
        in_specs=[SMEM, HBM, HBM, VMEM, HBM, HBM],
        out_specs=(HBM, HBM, HBM),
        scratch_shapes=[
            pltpu.VMEM((vocab, tokens), F32),
            pltpu.VMEM((vocab, tokens), F32),
            pltpu.VMEM((features, vocab), BF16),
            pltpu.VMEM((features, tokens), BF16),
            pltpu.VMEM((vocab, tokens), BF16),
            pltpu.VMEM((tokens, vocab), BF16),
            pltpu.VMEM((half, features), BF16),
            pltpu.VMEM((half, features), BF16),
            pltpu.VMEM((features, vocab), BF16),
            pltpu.SemaphoreType.DMA((4,)),
            pltpu.SemaphoreType.DMA((2 + NX,)),
        ],
        compiler_params=pltpu.CompilerParams(vmem_limit_bytes=GRANT),
        cost_estimate=pl.CostEstimate(
            flops=4 * vocab * tokens * features,
            bytes_accessed=10 << 20,
            transcendentals=2 * vocab * tokens,
        ),
    )(which, student, teacher, lse, weights, normed)


def added_kernel(left_ref, right_ref, out_ref):
    out_ref[...] = (left_ref[...].astype(F32) + right_ref[...].astype(F32)).astype(BF16)


def added(left, right):
    rows, columns = left.shape
    spec = pl.BlockSpec((rows // NX, columns), lambda i: (i, 0))
    return pl.pallas_call(
        added_kernel,
        out_shape=jax.ShapeDtypeStruct(left.shape, BF16),
        grid=(NX,),
        in_specs=[spec, spec],
        out_specs=spec,
        compiler_params=pltpu.CompilerParams(vmem_limit_bytes=16 << 20),
    )(left, right)


def squares_kernel(parts_ref, row_ref, head_ref, out_ref):
    head = jnp.sum(parts_ref[...].astype(F32), axis=0)
    head_ref[...] = head
    row = row_ref[...].astype(F32)
    lane = lax.broadcasted_iota(jnp.int32, out_ref.shape, 1)
    out_ref[...] = jnp.where(lane < 64, jnp.sum(head * head), jnp.sum(row * row))


def updates_kernel(devices, squares_ref, head_ref, row_ref, head_out, row_out):
    squares = jnp.sum(squares_ref[...], axis=0, keepdims=True)
    head = head_ref[...]
    row = row_ref[...].astype(F32)
    head_out[...] = (
        head * lax.rsqrt(squares[:, :1] / (head.size * devices) + epsilon)
    ).astype(BF16)
    row_out[...] = (
        row * lax.rsqrt(squares[:, 64:65] / (row.size * devices) + epsilon)
    ).astype(BF16)


def body(
    teacher_rows, teacher_gain, teacher_head, student_rows, student_gain, student_head, lengths
):
    fs = student_head.shape[1]
    vocab = teacher_head.shape[0]
    z = lax.axis_index("z")
    c = lax.axis_index("core")

    wide = teacher_rows.shape[1]
    sent = pl.pallas_call(
        scaled_kernel,
        out_shape=jax.ShapeDtypeStruct((wide + HEAD_ROWS, teacher_rows.shape[0]), BF16),
    )(teacher_rows.T, teacher_gain[None])
    rows = lax.all_gather(sent, ("core", "y"), axis=0, tiled=False)

    heads = jnp.concatenate([student_head.T, teacher_head.T], axis=0)
    own = lax.all_gather(heads, "x", axis=0, tiled=False)
    blocks, offsets = [own], [0]
    mine, theirs = own, swapped(own)
    for step in range(1, NZ // 2):
        mine, theirs = along(mine), along(theirs)
        if step < NZ // 2 - 1:
            blocks += [mine, swapped(theirs)]
            offsets += [-step, step]

    normed = normalize(student_rows, student_gain).T
    early = len(blocks)
    blocks += [mine, along(mine)]
    offsets += [1 - NZ // 2, -NZ // 2]
    where = jnp.stack([z, 1 - 2 * c])
    student_logits, teacher_logits, scale, weights = most(
        where, rows, normed, blocks[:early], offsets[:early], wide, fs
    )
    theirs, student_logits, teacher_logits, scale, weights = lax.optimization_barrier(
        (theirs, student_logits, teacher_logits, scale, weights)
    )
    blocks.append(swapped(theirs))
    offsets.append(NZ // 2 - 1)
    student_logits, teacher_logits, lse, weights = last(
        where,
        rows,
        normed,
        blocks[early:],
        student_logits,
        teacher_logits,
        scale,
        weights,
        offsets[early:],
        fs,
    )
    student_w = weights.reshape(NX * NZ * fs, vocab)

    which = jnp.stack([c, lengths[0]])
    lse, which, normed = lax.optimization_barrier((lse, which, normed))
    lse = lax.all_to_all(lse, ("core", "y"), 0, 0, tiled=True)
    other, mine, head_part = gradient(
        which, student_logits, teacher_logits, lse, student_w, normed
    )

    other = swapped(other)
    mine = added(mine, other)
    row_grad = lax.psum_scatter(mine, "y", scatter_dimension=0, tiled=True)

    head_part = lax.all_to_all(head_part.reshape(NX, NZ * fs, vocab), "x", 0, 0, tiled=True)
    head_part = jnp.sum(head_part.astype(F32), axis=0).astype(BF16)
    head_part = lax.all_to_all(head_part.reshape(NZ, fs, vocab), "z", 0, 0, tiled=True)

    devices = NX * NZ * NC * NY
    head_grad, squares = pl.pallas_call(
        squares_kernel,
        out_shape=(
            jax.ShapeDtypeStruct((fs, vocab), F32),
            jax.ShapeDtypeStruct((devices, 128), F32),
        ),
    )(head_part, row_grad)
    squares = lax.all_to_all(squares, ("x", "z", "core", "y"), 0, 0, tiled=True)
    head_update, row_update = pl.pallas_call(
        lambda *refs: updates_kernel(devices, *refs),
        out_shape=(
            jax.ShapeDtypeStruct((fs, vocab), BF16),
            jax.ShapeDtypeStruct(row_grad.shape, BF16),
        ),
    )(squares, head_grad, row_grad)
    return (head_update.T, row_update)


def solution(mesh):
    mesh = Mesh(mesh.devices.reshape(NX, NZ, NC, NY), ("x", "z", "core", "y"))
    dp, mp = ("x", "z"), ("core", "y")
    placed = (P(dp, mp), P(mp), P(mp, dp), P(dp, None), P(), P(mp, dp), P(dp))
    return jax.shard_map(
        body,
        mesh=mesh,
        in_specs=placed,
        out_specs=(P(mp, dp), P(dp + mp, None)),
        check_vma=False,
    )
```

```python
import jax
import jax.numpy as jnp
from jax import lax
from jax.experimental import pallas as pl
from jax.experimental.pallas import tpu as pltpu
from jax.sharding import Mesh, PartitionSpec as P

F32 = jnp.float32
BF16 = jnp.bfloat16
DT = 5120
NX, NZ, NC, NY = 4, 8, 2, 8
epsilon = 1e-06
HEAD_ROWS = 16
LSE_ROWS = 2
GRANT = 60 << 20
HBM = pl.BlockSpec(memory_space=pltpu.HBM)
VMEM = pl.BlockSpec(memory_space=pltpu.VMEM)
SMEM = pl.BlockSpec(memory_space=pltpu.SMEM)


def split3(values):
    high = values.astype(BF16)
    rest = values - high.astype(F32)
    middle = rest.astype(BF16)
    low = (rest - middle.astype(F32)).astype(BF16)
    return high, middle, low


def normalize(rows, gain):
    values = rows.astype(F32)
    mean_square = jnp.mean(values * values, axis=-1, keepdims=True)
    return (values * lax.rsqrt(mean_square + epsilon) * gain.astype(F32)).astype(BF16)


def along(values, cross_in=False, cross_out=False):
    pairs = []
    for i in range(NZ):
        for c in range(NC):
            near, far = i, (i + 1 - 2 * c) % NZ
            pairs.append((near * NC + (c ^ cross_in), far * NC + (c ^ cross_out)))
    return lax.ppermute(values, ("z", "core"), pairs)


def swapped(values):
    return lax.ppermute(values, "core", [(0, 1), (1, 0)])


def against(left, right, dims):
    return lax.dot_general(left, right, (dims, ((), ())), preferred_element_type=F32)


def log_sum_exp(values):
    top = jnp.max(values, axis=0, keepdims=True)
    return top + jnp.log(jnp.sum(jnp.exp(values - top), axis=0, keepdims=True))


def place_of(where_ref, offset):
    return lax.rem(where_ref[0] + where_ref[1] * offset + NZ, NZ)


def begin(copies):
    for copy in copies:
        copy.start()
    return copies


def finish(copies):
    for copy in copies:
        copy.wait()


def block_copies(where_ref, offsets, fs, rows_ref, normed_ref, blocks, held, sems):
    rows, normed, student_w, teacher_w = held
    ft = teacher_w.shape[2]
    per_block = rows_ref.shape[0] // NX
    fold = NZ // per_block
    student, teacher = [], []
    for i, (block, offset) in enumerate(zip(blocks, offsets)):
        at = place_of(where_ref, offset)
        inner = pl.multiple_of(lax.rem(at, fold) * ft, 16)
        copy_sems = sems.at[i]
        student.append(
            pltpu.make_async_copy(block.at[:, pl.ds(0, fs)], student_w.at[:, i], copy_sems.at[0])
        )
        teacher.append(
            pltpu.make_async_copy(block.at[:, pl.ds(fs, ft)], teacher_w.at[:, i], copy_sems.at[1])
        )
        for k in range(NX):
            source = pl.multiple_of(k * NZ * fs + at * fs, 16)
            student.append(
                pltpu.make_async_copy(
                    normed_ref.at[pl.ds(source, fs)], normed.at[k, i], copy_sems.at[2 + k]
                )
            )
            teacher.append(
                pltpu.make_async_copy(
                    rows_ref.at[k * per_block + lax.div(at, fold), pl.ds(inner, ft)],
                    rows.at[k, i],
                    copy_sems.at[2 + NX + k],
                )
            )
    return student, teacher


def weights_copies(where_ref, offsets, student_w, weights_ref, sems):
    return [
        pltpu.make_async_copy(
            student_w.at[:, i], weights_ref.at[:, place_of(where_ref, offset)], sems.at[i]
        )
        for i, offset in enumerate(offsets)
    ]


def product(weights, rows):
    features = weights.shape[1] * weights.shape[2]
    total = None
    for k in range(NX):
        part = against(
            weights[k].reshape(features, weights.shape[3]),
            rows[k].reshape(features, rows.shape[3]),
            ((0,), (0,)),
        )
        total = part if total is None else total + part
    return total


def held_blocks(count, fs, ft, vocab, tokens):
    return [
        pltpu.VMEM((NX, count, ft, tokens), BF16),
        pltpu.VMEM((NX, count, fs, tokens), BF16),
        pltpu.VMEM((NX, count, fs, vocab), BF16),
        pltpu.VMEM((NX, count, ft, vocab), BF16),
        pltpu.VMEM((vocab, tokens), F32),
        pltpu.VMEM((vocab, tokens), F32),
        pltpu.SemaphoreType.DMA((count, 2 + 2 * NX)),
        pltpu.SemaphoreType.DMA((count,)),
        pltpu.SemaphoreType.DMA((4,)),
    ]


def most_kernel(offsets, wide, fs, where_ref, rows_ref, normed_ref, *refs):
    count = len(offsets)
    blocks, refs = refs[:count], refs[count:]
    student_ref, teacher_ref, scale_ref, weights_ref, squares = refs[:5]
    *held, student, teacher, sems, weights_sems, out_sems = refs[5:]
    first, second = block_copies(
        where_ref, offsets, fs, rows_ref, normed_ref, blocks, held, sems
    )
    square_copy = pltpu.make_async_copy(
        rows_ref.at[:, pl.ds(wide, HEAD_ROWS)], squares, out_sems.at[0]
    )
    begin(first + second + [square_copy])
    finish(first)
    out_copies = begin(weights_copies(where_ref, offsets, held[2], weights_ref, weights_sems))
    student[...] = product(held[2], held[1])
    out_copies.append(pltpu.make_async_copy(student, student_ref, out_sems.at[1]))
    out_copies[-1].start()
    finish(second)
    teacher[...] = product(held[3], held[0])
    out_copies.append(pltpu.make_async_copy(teacher, teacher_ref, out_sems.at[2]))
    out_copies[-1].start()
    square_copy.wait()
    square = jnp.sum(jnp.sum(squares[...].astype(F32), axis=0), axis=0, keepdims=True)
    scale_ref[...] = lax.rsqrt(square / DT + epsilon)
    finish(out_copies)


def most(where, rows, normed, blocks, offsets, wide, fs):
    vocab = blocks[0].shape[2]
    ft = blocks[0].shape[1] - fs
    parts, _, tokens = rows.shape

    def kernel(*refs):
        most_kernel(offsets, wide, fs, *refs)

    return pl.pallas_call(
        kernel,
        out_shape=(
            jax.ShapeDtypeStruct((vocab, tokens), F32),
            jax.ShapeDtypeStruct((vocab, tokens), F32),
            jax.ShapeDtypeStruct((1, tokens), F32),
            jax.ShapeDtypeStruct((NX, NZ, fs, vocab), BF16),
        ),
        in_specs=[SMEM, HBM, HBM] + [HBM] * len(blocks),
        out_specs=(HBM, HBM, VMEM, HBM),
        scratch_shapes=[pltpu.VMEM((parts, HEAD_ROWS, tokens), BF16)]
        + held_blocks(len(blocks), fs, ft, vocab, tokens),
        compiler_params=pltpu.CompilerParams(vmem_limit_bytes=GRANT),
        cost_estimate=pl.CostEstimate(
            flops=2 * vocab * tokens * NX * (ft + fs) * len(blocks),
            bytes_accessed=12 << 20,
            transcendentals=0,
        ),
    )(where, rows, normed, *blocks)


def last_kernel(offsets, fs, where_ref, rows_ref, normed_ref, student_part, teacher_part, *refs):
    count = len(offsets)
    scale_ref, _, *blocks = refs[: 2 + count]
    student_ref, teacher_ref, lse_ref, weights_ref = refs[2 + count : 6 + count]
    *held, student, teacher, sems, weights_sems, out_sems = refs[6 + count :]
    first, second = block_copies(
        where_ref, offsets, fs, rows_ref, normed_ref, blocks, held, sems
    )
    first.append(pltpu.make_async_copy(student_part, student, out_sems.at[0]))
    second.append(pltpu.make_async_copy(teacher_part, teacher, out_sems.at[1]))
    begin(first + second)
    finish(first)
    out_copies = begin(weights_copies(where_ref, offsets, held[2], weights_ref, weights_sems))
    total = student[...] + product(held[2], held[1])
    student[...] = total
    out_copies.append(pltpu.make_async_copy(student, student_ref, out_sems.at[2]))
    out_copies[-1].start()
    student_lse = log_sum_exp(total)
    finish(second)
    total = scale_ref[...] * (teacher[...] + product(held[3], held[0]))
    teacher[...] = total
    out_copies.append(pltpu.make_async_copy(teacher, teacher_ref, out_sems.at[3]))
    out_copies[-1].start()
    both = jnp.concatenate([log_sum_exp(total), student_lse], axis=0)
    both = jnp.concatenate([both] * (lse_ref.shape[1] // 2), axis=0)
    lse_ref[...] = jnp.broadcast_to(both[None], lse_ref.shape)
    finish(out_copies)


def last(where, rows, normed, blocks, student, teacher, scale, weights, offsets, fs):
    vocab, tokens = student.shape
    ft = blocks[0].shape[1] - fs

    def kernel(*refs):
        last_kernel(offsets, fs, *refs)

    return pl.pallas_call(
        kernel,
        out_shape=(
            jax.ShapeDtypeStruct((vocab, tokens), F32),
            jax.ShapeDtypeStruct((vocab, tokens), F32),
            jax.ShapeDtypeStruct((NC * NY, LSE_ROWS, tokens), F32),
            jax.ShapeDtypeStruct(weights.shape, BF16),
        ),
        in_specs=[SMEM, HBM, HBM, HBM, HBM, VMEM] + [HBM] * (1 + len(blocks)),
        out_specs=(HBM, HBM, VMEM, HBM),
        input_output_aliases={6: 3},
        scratch_shapes=held_blocks(len(blocks), fs, ft, vocab, tokens),
        compiler_params=pltpu.CompilerParams(vmem_limit_bytes=GRANT),
        cost_estimate=pl.CostEstimate(
            flops=2 * vocab * tokens * NX * (ft + fs) * len(blocks),
            bytes_accessed=8 << 20,
            transcendentals=2 * vocab * tokens,
        ),
    )(where, rows, normed, student, teacher, scale, weights, *blocks)


def grad_kernel(which_ref, student_hbm, teacher_hbm, lse_ref, weights_hbm, normed_hbm, *refs):
    other_hbm, mine_hbm, head_hbm = refs[:3]
    student, teacher, weights, normed, grad_t, turned, other, mine, head, sems, out_sems = refs[3:]
    copies = begin(
        [
            pltpu.make_async_copy(source, held, sems.at[k])
            for k, (source, held) in enumerate(
                [
                    (student_hbm, student),
                    (teacher_hbm, teacher),
                    (weights_hbm, weights),
                    (normed_hbm, normed),
                ]
            )
        ]
    )
    tokens = student.shape[1]
    lses = lse_ref[:, 0:2]
    top = jnp.max(lses, axis=0)
    lse = top + jnp.log(jnp.sum(jnp.exp(lses - top[None]), axis=0))
    position = lax.broadcasted_iota(jnp.int32, (1, tokens), 1)
    live = (position < which_ref[1]).astype(F32)
    finish(copies[:2])
    grad = live * (jnp.exp(student[...] - lse[1:2]) - jnp.exp(teacher[...] - lse[0:1]))
    grad_t[...] = grad.astype(BF16)
    turned[...] = grad_t[...].T
    half = tokens // NC
    core = which_ref[0]
    parts = [
        (other, other_hbm, turned[pl.ds(pl.multiple_of((1 - core) * half, half), half), :]),
        (mine, mine_hbm, turned[pl.ds(pl.multiple_of(core * half, half), half), :]),
    ]
    width = weights.shape[0] // NX
    slices = [pl.ds(k * width, width) for k in range(NX)]
    copies[2].wait()
    out_copies = []
    for i, (out, hbm, block) in enumerate(parts):
        for columns in slices:
            out[:, columns] = against(block, weights[columns, :], ((1,), (1,))).astype(BF16)
        out_copies.append(pltpu.make_async_copy(out, hbm, out_sems.at[i]))
        out_copies[-1].start()
    copies[3].wait()
    for k, rows in enumerate(slices):
        head[rows, :] = against(normed[rows, :], grad_t[...], ((1,), (1,))).astype(BF16)
        out_copies.append(pltpu.make_async_copy(head.at[rows], head_hbm.at[rows], out_sems.at[2 + k]))
        out_copies[-1].start()
    finish(out_copies)


def gradient(which, student, teacher, lse, weights, normed):
    vocab, tokens = student.shape
    features = weights.shape[0]
    half = tokens // NC
    return pl.pallas_call(
        grad_kernel,
        out_shape=(
            jax.ShapeDtypeStruct((half, features), BF16),
            jax.ShapeDtypeStruct((half, features), BF16),
            jax.ShapeDtypeStruct((features, vocab), BF16),
        ),
        in_specs=[SMEM, HBM, HBM, VMEM, HBM, HBM],
        out_specs=(HBM, HBM, HBM),
        scratch_shapes=[
            pltpu.VMEM((vocab, tokens), F32),
            pltpu.VMEM((vocab, tokens), F32),
            pltpu.VMEM((features, vocab), BF16),
            pltpu.VMEM((features, tokens), BF16),
            pltpu.VMEM((vocab, tokens), BF16),
            pltpu.VMEM((tokens, vocab), BF16),
            pltpu.VMEM((half, features), BF16),
            pltpu.VMEM((half, features), BF16),
            pltpu.VMEM((features, vocab), BF16),
            pltpu.SemaphoreType.DMA((4,)),
            pltpu.SemaphoreType.DMA((2 + NX,)),
        ],
        compiler_params=pltpu.CompilerParams(vmem_limit_bytes=GRANT),
        cost_estimate=pl.CostEstimate(
            flops=4 * vocab * tokens * features,
            bytes_accessed=10 << 20,
            transcendentals=2 * vocab * tokens,
        ),
    )(which, student, teacher, lse, weights, normed)


def added_kernel(left_ref, right_ref, out_ref):
    out_ref[...] = (left_ref[...].astype(F32) + right_ref[...].astype(F32)).astype(BF16)


def added(left, right):
    rows, columns = left.shape
    spec = pl.BlockSpec((rows // NX, columns), lambda i: (i, 0))
    return pl.pallas_call(
        added_kernel,
        out_shape=jax.ShapeDtypeStruct(left.shape, BF16),
        grid=(NX,),
        in_specs=[spec, spec],
        out_specs=spec,
        compiler_params=pltpu.CompilerParams(vmem_limit_bytes=16 << 20),
    )(left, right)


def squares_kernel(parts_ref, row_ref, head_ref, out_ref):
    head = jnp.sum(parts_ref[...].astype(F32), axis=0)
    head_ref[...] = head
    row = row_ref[...].astype(F32)
    lane = lax.broadcasted_iota(jnp.int32, out_ref.shape, 1)
    out_ref[...] = jnp.where(lane < 64, jnp.sum(head * head), jnp.sum(row * row))


def updates_kernel(devices, squares_ref, head_ref, row_ref, head_out, row_out):
    squares = jnp.sum(squares_ref[...], axis=0, keepdims=True)
    head = head_ref[...]
    row = row_ref[...].astype(F32)
    head_out[...] = (
        head * lax.rsqrt(squares[:, :1] / (head.size * devices) + epsilon)
    ).astype(BF16)
    row_out[...] = (
        row * lax.rsqrt(squares[:, 64:65] / (row.size * devices) + epsilon)
    ).astype(BF16)


def body(
    teacher_rows, teacher_gain, teacher_head, student_rows, student_gain, student_head, lengths
):
    fs = student_head.shape[1]
    vocab = teacher_head.shape[0]
    z = lax.axis_index("z")
    c = lax.axis_index("core")

    block = teacher_rows.T
    wide = block.shape[0]
    values = block.astype(F32)
    scaled = (values * teacher_gain.astype(F32)[:, None]).astype(BF16)
    squares = jnp.stack(split3(jnp.sum(values * values, axis=0)), axis=0)
    sent = jnp.concatenate([scaled, jnp.pad(squares, ((0, HEAD_ROWS - 3), (0, 0)))], axis=0)
    rows = lax.all_gather(sent, ("core", "y"), axis=0, tiled=False)

    heads = jnp.concatenate([student_head.T, teacher_head.T], axis=0)
    own = lax.all_gather(heads, "x", axis=0, tiled=False)
    blocks, offsets = [own], [0]
    mine = theirs = own
    for step in range(1, NZ // 2):
        final = step == NZ // 2 - 1
        mine, theirs = along(mine), along(theirs, cross_in=step == 1, cross_out=final)
        blocks.append(mine)
        offsets.append(-step)
        if not final:
            blocks.append(swapped(theirs))
            offsets.append(step)

    normed = normalize(student_rows, student_gain).T
    early = len(blocks)
    blocks += [theirs, along(mine)]
    offsets += [NZ // 2 - 1, -NZ // 2]
    where = jnp.stack([z, 1 - 2 * c])
    student_logits, teacher_logits, scale, weights = most(
        where, rows, normed, blocks[:early], offsets[:early], wide, fs
    )
    student_logits, teacher_logits, lse, weights = last(
        where,
        rows,
        normed,
        blocks[early:],
        student_logits,
        teacher_logits,
        scale,
        weights,
        offsets[early:],
        fs,
    )
    student_w = weights.reshape(NX * NZ * fs, vocab)

    which = jnp.stack([c, lengths[0]])
    lse, which, normed = lax.optimization_barrier((lse, which, normed))
    lse = lax.all_to_all(lse, ("core", "y"), 0, 0, tiled=True)
    other, mine, head_part = gradient(
        which, student_logits, teacher_logits, lse, student_w, normed
    )

    other = swapped(other)
    mine = added(mine, other)
    row_grad = lax.psum_scatter(mine, "y", scatter_dimension=0, tiled=True)

    head_part = lax.all_to_all(head_part.reshape(NX, NZ * fs, vocab), "x", 0, 0, tiled=True)
    head_part = jnp.sum(head_part.astype(F32), axis=0).astype(BF16)
    head_part = lax.all_to_all(head_part.reshape(NZ, fs, vocab), "z", 0, 0, tiled=True)

    devices = NX * NZ * NC * NY
    head_grad, squares = pl.pallas_call(
        squares_kernel,
        out_shape=(
            jax.ShapeDtypeStruct((fs, vocab), F32),
            jax.ShapeDtypeStruct((devices, 128), F32),
        ),
    )(head_part, row_grad)
    squares = lax.all_to_all(squares, ("x", "z", "core", "y"), 0, 0, tiled=True)
    head_update, row_update = pl.pallas_call(
        lambda *refs: updates_kernel(devices, *refs),
        out_shape=(
            jax.ShapeDtypeStruct((fs, vocab), BF16),
            jax.ShapeDtypeStruct(row_grad.shape, BF16),
        ),
    )(squares, head_grad, row_grad)
    return (head_update.T, row_update)


def solution(mesh):
    mesh = Mesh(mesh.devices.reshape(NX, NZ, NC, NY), ("x", "z", "core", "y"))
    dp, mp = ("x", "z"), ("core", "y")
    placed = (P(dp, mp), P(mp), P(mp, dp), P(dp, None), P(), P(mp, dp), P(dp))
    return jax.shard_map(
        body,
        mesh=mesh,
        in_specs=placed,
        out_specs=(P(mp, dp), P(dp + mp, None)),
        check_vma=False,
    )
```

```python
import jax
import jax.numpy as jnp
from jax import lax
from jax.experimental import pallas as pl
from jax.experimental.pallas import tpu as pltpu
from jax.sharding import Mesh, PartitionSpec as P

F32 = jnp.float32
BF16 = jnp.bfloat16
DT = 5120
NX, NZ, NC, NY = 4, 8, 2, 8
epsilon = 1e-06
HEAD_ROWS = 16
LSE_ROWS = 2
GRANT = 60 << 20
HBM = pl.BlockSpec(memory_space=pltpu.HBM)
VMEM = pl.BlockSpec(memory_space=pltpu.VMEM)
SMEM = pl.BlockSpec(memory_space=pltpu.SMEM)


def split3(values):
    high = values.astype(BF16)
    rest = values - high.astype(F32)
    middle = rest.astype(BF16)
    low = (rest - middle.astype(F32)).astype(BF16)
    return high, middle, low


def normalize(rows, gain):
    values = rows.astype(F32)
    mean_square = jnp.mean(values * values, axis=-1, keepdims=True)
    return (values * lax.rsqrt(mean_square + epsilon) * gain.astype(F32)).astype(BF16)


def along(values, cross_in=False, cross_out=False):
    pairs = []
    for i in range(NZ):
        for c in range(NC):
            near, far = i, (i + 1 - 2 * c) % NZ
            pairs.append((near * NC + (c ^ cross_in), far * NC + (c ^ cross_out)))
    return lax.ppermute(values, ("z", "core"), pairs)


def swapped(values):
    return lax.ppermute(values, "core", [(0, 1), (1, 0)])


def against(left, right, dims):
    return lax.dot_general(left, right, (dims, ((), ())), preferred_element_type=F32)


def log_sum_exp(values):
    top = jnp.max(values, axis=0, keepdims=True)
    return top + jnp.log(jnp.sum(jnp.exp(values - top), axis=0, keepdims=True))


def place_of(where_ref, offset):
    return lax.rem(where_ref[0] + where_ref[1] * offset + NZ, NZ)


def begin(copies):
    for copy in copies:
        copy.start()
    return copies


def finish(copies):
    for copy in copies:
        copy.wait()


def block_copies(where_ref, offsets, fs, rows_ref, normed_ref, blocks, held, sems):
    rows, normed, student_w, teacher_w = held
    ft = teacher_w.shape[2]
    per_block = rows_ref.shape[0] // NX
    fold = NZ // per_block
    student, teacher = [], []
    for i, (block, offset) in enumerate(zip(blocks, offsets)):
        at = place_of(where_ref, offset)
        inner = pl.multiple_of(lax.rem(at, fold) * ft, 16)
        copy_sems = sems.at[i]
        student.append(
            pltpu.make_async_copy(block.at[:, pl.ds(0, fs)], student_w.at[:, i], copy_sems.at[0])
        )
        teacher.append(
            pltpu.make_async_copy(block.at[:, pl.ds(fs, ft)], teacher_w.at[:, i], copy_sems.at[1])
        )
        for k in range(NX):
            source = pl.multiple_of(k * NZ * fs + at * fs, 16)
            student.append(
                pltpu.make_async_copy(
                    normed_ref.at[pl.ds(source, fs)], normed.at[k, i], copy_sems.at[2 + k]
                )
            )
            teacher.append(
                pltpu.make_async_copy(
                    rows_ref.at[k * per_block + lax.div(at, fold), pl.ds(inner, ft)],
                    rows.at[k, i],
                    copy_sems.at[2 + NX + k],
                )
            )
    return student, teacher


def weights_copies(where_ref, offsets, student_w, weights_ref, sems):
    return [
        pltpu.make_async_copy(
            student_w.at[:, i], weights_ref.at[:, place_of(where_ref, offset)], sems.at[i]
        )
        for i, offset in enumerate(offsets)
    ]


def product(weights, rows):
    features = weights.shape[1] * weights.shape[2]
    total = None
    for k in range(NX):
        part = against(
            weights[k].reshape(features, weights.shape[3]),
            rows[k].reshape(features, rows.shape[3]),
            ((0,), (0,)),
        )
        total = part if total is None else total + part
    return total


def held_blocks(count, fs, ft, vocab, tokens):
    return [
        pltpu.VMEM((NX, count, ft, tokens), BF16),
        pltpu.VMEM((NX, count, fs, tokens), BF16),
        pltpu.VMEM((NX, count, fs, vocab), BF16),
        pltpu.VMEM((NX, count, ft, vocab), BF16),
        pltpu.VMEM((vocab, tokens), F32),
        pltpu.VMEM((vocab, tokens), F32),
        pltpu.SemaphoreType.DMA((count, 2 + 2 * NX)),
        pltpu.SemaphoreType.DMA((count,)),
        pltpu.SemaphoreType.DMA((4,)),
    ]


def most_kernel(offsets, wide, fs, where_ref, rows_ref, normed_ref, *refs):
    count = len(offsets)
    blocks, refs = refs[:count], refs[count:]
    student_ref, teacher_ref, scale_ref, weights_ref, squares = refs[:5]
    *held, student, teacher, sems, weights_sems, out_sems = refs[5:]
    first, second = block_copies(
        where_ref, offsets, fs, rows_ref, normed_ref, blocks, held, sems
    )
    square_copy = pltpu.make_async_copy(
        rows_ref.at[:, pl.ds(wide, HEAD_ROWS)], squares, out_sems.at[0]
    )
    begin(first + second + [square_copy])
    finish(first)
    out_copies = begin(weights_copies(where_ref, offsets, held[2], weights_ref, weights_sems))
    student[...] = product(held[2], held[1])
    out_copies.append(pltpu.make_async_copy(student, student_ref, out_sems.at[1]))
    out_copies[-1].start()
    finish(second)
    teacher[...] = product(held[3], held[0])
    out_copies.append(pltpu.make_async_copy(teacher, teacher_ref, out_sems.at[2]))
    out_copies[-1].start()
    square_copy.wait()
    square = jnp.sum(jnp.sum(squares[...].astype(F32), axis=0), axis=0, keepdims=True)
    scale_ref[...] = lax.rsqrt(square / DT + epsilon)
    finish(out_copies)


def most(where, rows, normed, blocks, offsets, wide, fs):
    vocab = blocks[0].shape[2]
    ft = blocks[0].shape[1] - fs
    parts, _, tokens = rows.shape

    def kernel(*refs):
        most_kernel(offsets, wide, fs, *refs)

    return pl.pallas_call(
        kernel,
        out_shape=(
            jax.ShapeDtypeStruct((vocab, tokens), F32),
            jax.ShapeDtypeStruct((vocab, tokens), F32),
            jax.ShapeDtypeStruct((1, tokens), F32),
            jax.ShapeDtypeStruct((NX, NZ, fs, vocab), BF16),
        ),
        in_specs=[SMEM, HBM, HBM] + [HBM] * len(blocks),
        out_specs=(HBM, HBM, VMEM, HBM),
        scratch_shapes=[pltpu.VMEM((parts, HEAD_ROWS, tokens), BF16)]
        + held_blocks(len(blocks), fs, ft, vocab, tokens),
        compiler_params=pltpu.CompilerParams(vmem_limit_bytes=GRANT),
        cost_estimate=pl.CostEstimate(
            flops=2 * vocab * tokens * NX * (ft + fs) * len(blocks),
            bytes_accessed=12 << 20,
            transcendentals=0,
        ),
    )(where, rows, normed, *blocks)


def last_kernel(offsets, fs, where_ref, rows_ref, normed_ref, student_part, teacher_part, *refs):
    count = len(offsets)
    scale_ref, _, *blocks = refs[: 2 + count]
    student_ref, teacher_ref, lse_ref, weights_ref = refs[2 + count : 6 + count]
    *held, student, teacher, sems, weights_sems, out_sems = refs[6 + count :]
    first, second = block_copies(
        where_ref, offsets, fs, rows_ref, normed_ref, blocks, held, sems
    )
    first.append(pltpu.make_async_copy(student_part, student, out_sems.at[0]))
    second.append(pltpu.make_async_copy(teacher_part, teacher, out_sems.at[1]))
    begin(first + second)
    finish(first)
    out_copies = begin(weights_copies(where_ref, offsets, held[2], weights_ref, weights_sems))
    total = student[...] + product(held[2], held[1])
    student[...] = total
    out_copies.append(pltpu.make_async_copy(student, student_ref, out_sems.at[2]))
    out_copies[-1].start()
    student_lse = log_sum_exp(total)
    finish(second)
    total = scale_ref[...] * (teacher[...] + product(held[3], held[0]))
    teacher[...] = total
    out_copies.append(pltpu.make_async_copy(teacher, teacher_ref, out_sems.at[3]))
    out_copies[-1].start()
    both = jnp.concatenate([log_sum_exp(total), student_lse], axis=0)
    both = jnp.concatenate([both] * (lse_ref.shape[1] // 2), axis=0)
    lse_ref[...] = jnp.broadcast_to(both[None], lse_ref.shape)
    finish(out_copies)


def last(where, rows, normed, blocks, student, teacher, scale, weights, offsets, fs):
    vocab, tokens = student.shape
    ft = blocks[0].shape[1] - fs

    def kernel(*refs):
        last_kernel(offsets, fs, *refs)

    return pl.pallas_call(
        kernel,
        out_shape=(
            jax.ShapeDtypeStruct((vocab, tokens), F32),
            jax.ShapeDtypeStruct((vocab, tokens), F32),
            jax.ShapeDtypeStruct((NC * NY, LSE_ROWS, tokens), F32),
            jax.ShapeDtypeStruct(weights.shape, BF16),
        ),
        in_specs=[SMEM, HBM, HBM, HBM, HBM, VMEM] + [HBM] * (1 + len(blocks)),
        out_specs=(HBM, HBM, VMEM, HBM),
        input_output_aliases={6: 3},
        scratch_shapes=held_blocks(len(blocks), fs, ft, vocab, tokens),
        compiler_params=pltpu.CompilerParams(vmem_limit_bytes=GRANT),
        cost_estimate=pl.CostEstimate(
            flops=2 * vocab * tokens * NX * (ft + fs) * len(blocks),
            bytes_accessed=8 << 20,
            transcendentals=2 * vocab * tokens,
        ),
    )(where, rows, normed, student, teacher, scale, weights, *blocks)


def grad_kernel(which_ref, student_hbm, teacher_hbm, lse_ref, weights_hbm, normed_hbm, *refs):
    other_hbm, mine_hbm, head_hbm = refs[:3]
    student, teacher, weights, normed, grad_t, turned, other, mine, head, sems, out_sems = refs[3:]
    copies = begin(
        [
            pltpu.make_async_copy(source, held, sems.at[k])
            for k, (source, held) in enumerate(
                [
                    (student_hbm, student),
                    (teacher_hbm, teacher),
                    (weights_hbm, weights),
                    (normed_hbm, normed),
                ]
            )
        ]
    )
    tokens = student.shape[1]
    lses = lse_ref[:, 0:2]
    top = jnp.max(lses, axis=0)
    lse = top + jnp.log(jnp.sum(jnp.exp(lses - top[None]), axis=0))
    position = lax.broadcasted_iota(jnp.int32, (1, tokens), 1)
    live = (position < which_ref[1]).astype(F32)
    finish(copies[:2])
    grad = live * (jnp.exp(student[...] - lse[1:2]) - jnp.exp(teacher[...] - lse[0:1]))
    grad_t[...] = grad.astype(BF16)
    turned[...] = grad_t[...].T
    half = tokens // NC
    core = which_ref[0]
    parts = [
        (other, other_hbm, turned[pl.ds(pl.multiple_of((1 - core) * half, half), half), :]),
        (mine, mine_hbm, turned[pl.ds(pl.multiple_of(core * half, half), half), :]),
    ]
    width = weights.shape[0] // NX
    slices = [pl.ds(k * width, width) for k in range(NX)]
    copies[2].wait()
    out_copies = []
    for i, (out, hbm, block) in enumerate(parts):
        for columns in slices:
            out[:, columns] = against(block, weights[columns, :], ((1,), (1,))).astype(BF16)
        out_copies.append(pltpu.make_async_copy(out, hbm, out_sems.at[i]))
        out_copies[-1].start()
    copies[3].wait()
    for k, rows in enumerate(slices):
        head[rows, :] = against(normed[rows, :], grad_t[...], ((1,), (1,))).astype(BF16)
        out_copies.append(pltpu.make_async_copy(head.at[rows], head_hbm.at[rows], out_sems.at[2 + k]))
        out_copies[-1].start()
    finish(out_copies)


def gradient(which, student, teacher, lse, weights, normed):
    vocab, tokens = student.shape
    features = weights.shape[0]
    half = tokens // NC
    return pl.pallas_call(
        grad_kernel,
        out_shape=(
            jax.ShapeDtypeStruct((half, features), BF16),
            jax.ShapeDtypeStruct((half, features), BF16),
            jax.ShapeDtypeStruct((features, vocab), BF16),
        ),
        in_specs=[SMEM, HBM, HBM, VMEM, HBM, HBM],
        out_specs=(HBM, HBM, HBM),
        scratch_shapes=[
            pltpu.VMEM((vocab, tokens), F32),
            pltpu.VMEM((vocab, tokens), F32),
            pltpu.VMEM((features, vocab), BF16),
            pltpu.VMEM((features, tokens), BF16),
            pltpu.VMEM((vocab, tokens), BF16),
            pltpu.VMEM((tokens, vocab), BF16),
            pltpu.VMEM((half, features), BF16),
            pltpu.VMEM((half, features), BF16),
            pltpu.VMEM((features, vocab), BF16),
            pltpu.SemaphoreType.DMA((4,)),
            pltpu.SemaphoreType.DMA((2 + NX,)),
        ],
        compiler_params=pltpu.CompilerParams(vmem_limit_bytes=GRANT),
        cost_estimate=pl.CostEstimate(
            flops=4 * vocab * tokens * features,
            bytes_accessed=10 << 20,
            transcendentals=2 * vocab * tokens,
        ),
    )(which, student, teacher, lse, weights, normed)


def added_kernel(left_ref, right_ref, out_ref):
    out_ref[...] = (left_ref[...].astype(F32) + right_ref[...].astype(F32)).astype(BF16)


def added(left, right):
    rows, columns = left.shape
    spec = pl.BlockSpec((rows // NX, columns), lambda i: (i, 0))
    return pl.pallas_call(
        added_kernel,
        out_shape=jax.ShapeDtypeStruct(left.shape, BF16),
        grid=(NX,),
        in_specs=[spec, spec],
        out_specs=spec,
        compiler_params=pltpu.CompilerParams(vmem_limit_bytes=16 << 20),
    )(left, right)


def squares_kernel(parts_ref, row_ref, head_ref, out_ref):
    head = jnp.sum(parts_ref[...].astype(F32), axis=0)
    head_ref[...] = head
    row = row_ref[...].astype(F32)
    lane = lax.broadcasted_iota(jnp.int32, out_ref.shape, 1)
    out_ref[...] = jnp.where(lane < 64, jnp.sum(head * head), jnp.sum(row * row))


def updates_kernel(devices, squares_ref, head_ref, row_ref, head_out, row_out):
    squares = jnp.sum(squares_ref[...], axis=0, keepdims=True)
    head = head_ref[...]
    row = row_ref[...].astype(F32)
    head_out[...] = (
        head * lax.rsqrt(squares[:, :1] / (head.size * devices) + epsilon)
    ).astype(BF16)
    row_out[...] = (
        row * lax.rsqrt(squares[:, 64:65] / (row.size * devices) + epsilon)
    ).astype(BF16)


def body(
    teacher_rows, teacher_gain, teacher_head, student_rows, student_gain, student_head, lengths
):
    fs = student_head.shape[1]
    vocab = teacher_head.shape[0]
    z = lax.axis_index("z")
    c = lax.axis_index("core")

    block = teacher_rows.T
    wide = block.shape[0]
    values = block.astype(F32)
    scaled = (values * teacher_gain.astype(F32)[:, None]).astype(BF16)
    squares = jnp.stack(split3(jnp.sum(values * values, axis=0)), axis=0)
    sent = jnp.concatenate([scaled, jnp.pad(squares, ((0, HEAD_ROWS - 3), (0, 0)))], axis=0)
    rows = lax.all_gather(sent, ("core", "y"), axis=0, tiled=False)

    heads = jnp.concatenate([student_head.T, teacher_head.T], axis=0)
    own = lax.all_gather(heads, "x", axis=0, tiled=False)
    blocks, offsets = [own], [0]
    normed = normalize(student_rows, student_gain).T
    mine, (theirs, normed) = own, lax.optimization_barrier((own, normed))
    for step in range(1, NZ // 2):
        final = step == NZ // 2 - 1
        mine, theirs = along(mine), along(theirs, cross_in=step == 1, cross_out=final)
        blocks.append(mine)
        offsets.append(-step)
        if not final:
            blocks.append(swapped(theirs))
            offsets.append(step)

    early = len(blocks)
    blocks += [theirs, along(mine)]
    offsets += [NZ // 2 - 1, -NZ // 2]
    where = jnp.stack([z, 1 - 2 * c])
    student_logits, teacher_logits, scale, weights = most(
        where, rows, normed, blocks[:early], offsets[:early], wide, fs
    )
    student_logits, teacher_logits, lse, weights = last(
        where,
        rows,
        normed,
        blocks[early:],
        student_logits,
        teacher_logits,
        scale,
        weights,
        offsets[early:],
        fs,
    )
    student_w = weights.reshape(NX * NZ * fs, vocab)

    which = jnp.stack([c, lengths[0]])
    lse, which, normed = lax.optimization_barrier((lse, which, normed))
    lse = lax.all_to_all(lse, ("core", "y"), 0, 0, tiled=True)
    other, mine, head_part = gradient(
        which, student_logits, teacher_logits, lse, student_w, normed
    )

    other = swapped(other)
    mine = added(mine, other)
    row_grad = lax.psum_scatter(mine, "y", scatter_dimension=0, tiled=True)

    head_part = lax.all_to_all(head_part.reshape(NX, NZ * fs, vocab), "x", 0, 0, tiled=True)
    head_part = jnp.sum(head_part.astype(F32), axis=0).astype(BF16)
    head_part = lax.all_to_all(head_part.reshape(NZ, fs, vocab), "z", 0, 0, tiled=True)

    devices = NX * NZ * NC * NY
    head_grad, squares = pl.pallas_call(
        squares_kernel,
        out_shape=(
            jax.ShapeDtypeStruct((fs, vocab), F32),
            jax.ShapeDtypeStruct((devices, 128), F32),
        ),
    )(head_part, row_grad)
    squares = lax.all_to_all(squares, ("x", "z", "core", "y"), 0, 0, tiled=True)
    head_update, row_update = pl.pallas_call(
        lambda *refs: updates_kernel(devices, *refs),
        out_shape=(
            jax.ShapeDtypeStruct((fs, vocab), BF16),
            jax.ShapeDtypeStruct(row_grad.shape, BF16),
        ),
    )(squares, head_grad, row_grad)
    return (head_update.T, row_update)


def solution(mesh):
    mesh = Mesh(mesh.devices.reshape(NX, NZ, NC, NY), ("x", "z", "core", "y"))
    dp, mp = ("x", "z"), ("core", "y")
    placed = (P(dp, mp), P(mp), P(mp, dp), P(dp, None), P(), P(mp, dp), P(dp))
    return jax.shard_map(
        body,
        mesh=mesh,
        in_specs=placed,
        out_specs=(P(mp, dp), P(dp + mp, None)),
        check_vma=False,
    )
```
